128 devices in a mesh: dp: 2 (over y_hi), seq: 16 (over z, x), chan: 4 (over y_lo, core).
Axes of the slice: x: 4, y: 4 (y_hi: 2, y_lo: 2; y = y_hi * 2 + y_lo), z: 4, core: 2. Of those that a mesh axis runs over, the one named last changes fastest.
Arguments:
- inputs: float32 [2, 256, 16384], P('dp', 'chan', 'seq'), may hold values from -6 to 6
- cotangent: float32 [2, 256, 16384], P('dp', 'chan', 'seq'), may hold values from -6 to 6
- conv_weight: float32 [3, 256], P(None, 'chan'), may hold values from -3.5 to 3.5
- kernel: float32 [256, 16384], P(('chan', 'seq')), may hold values from -3 to 3
- skip_gain: float32 [256], P(('chan', 'seq')), may hold values from 0.5 to 1.5
- mix_weight: float32 [256, 256], P(None, 'chan'), may hold values from -0.375 to 0.375
Outputs:
- outputs: float32 [2, 256, 16384], P('dp', 'chan', 'seq')
- grad_inputs: float32 [2, 256, 16384], P('dp', 'chan', 'seq')
- grad_kernel: float32 [256, 16384], P(('chan', 'seq'))
- grad_skip: float32 [256], P(('chan', 'seq'))
- grad_mix: float32 [256, 256], P(None, 'chan')
- grad_conv: float32 [3, 256], P(None, 'chan')
The draws below stay inside these ranges and needn't reach their ends.
All inputs are finite; a program needn't handle non-finite values.
Results may differ from the reference program's by a relative error of at most 0.00028.
Values sent between devices are 32-bit elements; how exact they have to be, the bound alone decides.
No kernel may reach another device: no remote copies, remote signals or barrier semaphores. Data moves between devices by JAX's collectives and lax.ppermute only.
A program may use at most 128 MiB of HBM per device.

```python
import jax
import jax.numpy as jnp
from jax import lax

H = 256
BATCH = 2
L = 16384


def draw_kernel(key, part):
    key = jax.random.fold_in(key, 11)
    keys = jax.random.split(key, 4)
    share = 0.5
    noise = jnp.clip(jax.random.normal(keys[3], (H, L), jnp.float32), -5.0, 5.0)
    slow = jax.random.uniform(keys[0], (H, 1), jnp.float32) < share
    slow_rate = jnp.exp(jax.random.uniform(keys[1], (H, 1), jnp.float32, jnp.log(0.1 / L), jnp.log(2.0 / L)))
    fast_rate = jnp.exp(jax.random.uniform(keys[2], (H, 1), jnp.float32, jnp.log(1.0 / 50.0), jnp.log(1.0 / 10.0)))
    rate = jnp.where(slow, slow_rate, fast_rate)
    steps = jnp.arange(L, dtype=jnp.float32)[None, :]
    envelope = jnp.exp(-rate * steps) * jnp.sqrt(1.0 - jnp.exp(-2.0 * rate))
    return (noise * envelope).astype(jnp.float32)


def steps_of(stream_key, dims, cuts, low, top_value):
    level, own = 1.0, jax.random.fold_in(stream_key, 6)
    for axis_at, shards_of in cuts:
        heights = jnp.exp(jax.random.uniform(jax.random.fold_in(own, axis_at), (shards_of,), jnp.float32, low / len(cuts), top_value / len(cuts)))
        level = level * jnp.repeat(heights, dims[axis_at] // shards_of).reshape([-1 if axis == axis_at else 1 for axis in range(len(dims))])
    return level


def normal_values(key, shape, deviation, reach, pieces=(), kind=jnp.bfloat16):
    result = deviation * jax.random.normal(key, shape, jnp.float32)
    if pieces:
        result = result * steps_of(key, shape, pieces, -0.22, 0.18)
    return jnp.clip(result, -reach, reach).astype(kind)


def setup_inputs(seed: int = 0) -> dict:
    streams_of = jax.random.split(jax.random.key(seed), 7)
    inputs = normal_values(streams_of[0], (BATCH, H, L), 1.0, 6.0, ((0, 2), (1, 4), (2, 16)), jnp.float32)
    cotangent = normal_values(streams_of[1], (BATCH, H, L), 1.0, 6.0, ((0, 2), (1, 4), (2, 16)), jnp.float32)
    conv_weight = normal_values(streams_of[2], (3, H), 3 ** -0.5, 3.5, ((1, 4),), jnp.float32)
    kernel = draw_kernel(jax.random.fold_in(streams_of[6], 71), 0)
    skip_gain = jnp.clip(0.5 + 1.0 * jax.random.uniform(streams_of[4], (H,), jnp.float32) ** steps_of(streams_of[4], (H,), ((0, 64),), -0.2, 0.2), 0.5, 1.5)
    mix_weight = normal_values(streams_of[5], (H, H), H ** -0.5, 0.375, ((1, 4),), jnp.float32)
    return {"inputs": inputs, "cotangent": cotangent, "conv_weight": conv_weight, "kernel": kernel, "skip_gain": skip_gain, "mix_weight": mix_weight}


def forward(inputs, conv_weight, kernel, skip_gain, mix_weight):
    length = inputs.shape[2]
    padded = jnp.pad(inputs, ((0, 0), (0, 0), (2, 0)))
    conv = conv_weight[0][None, :, None] * padded[:, :, :length]
    conv = conv + conv_weight[1][None, :, None] * padded[:, :, 1:length + 1]
    conv = conv + conv_weight[2][None, :, None] * padded[:, :, 2:]
    fsize = 2 * length
    spectrum = jnp.fft.rfft(conv, n=fsize) * jnp.fft.rfft(kernel, n=fsize)[None]
    long_out = jnp.fft.irfft(spectrum, n=fsize)[:, :, :length] + skip_gain[None, :, None] * conv
    activated = jax.nn.gelu(long_out)
    mixed = jnp.einsum('co,bct->bot', mix_weight, activated, precision=lax.Precision.HIGHEST)
    return inputs + mixed

def reference(inputs, cotangent, conv_weight, kernel, skip_gain, mix_weight):
    outputs, backward = jax.vjp(forward, inputs, conv_weight, kernel, skip_gain, mix_weight)
    grads = backward(cotangent)
    return (outputs, grads[0], grads[2], grads[3], grads[4], grads[1])
```

```python
import functools
import math

import jax
import jax.numpy as jnp
import ml_dtypes
import numpy as np
from jax import lax
from jax.experimental import pallas as pl
from jax.experimental.pallas import tpu as pltpu
from jax.sharding import PartitionSpec as P

SIDE = 128
LENGTH = SIDE * SIDE
F32 = jnp.float32
BF16 = jnp.bfloat16
GELU_SCALE = math.sqrt(2.0 / math.pi)
GELU_CUBE = 0.044715
VMEM = pl.BlockSpec(memory_space=pltpu.VMEM)
SMEM = pl.BlockSpec(memory_space=pltpu.SMEM)


def two_parts(table):
    high = table.astype(ml_dtypes.bfloat16)
    low = (table - high.astype(np.float64)).astype(ml_dtypes.bfloat16)
    return high, low


@functools.cache
def tables():
    one = np.arange(SIDE, dtype=np.float64)
    turn = 2.0 * np.pi * np.outer(one + 0.25, one) / SIDE
    rows = np.concatenate([np.cos(turn), -np.sin(turn)], axis=0)
    high, low = two_parts(rows)
    into_rows = np.concatenate([high, low, high], axis=1)
    high, low = two_parts(rows.T / LENGTH)
    back_rows = np.concatenate([high, low, high], axis=1)
    turn = 2.0 * np.pi * np.outer(one, one) / SIDE
    real, imag = np.cos(turn), -np.sin(turn)
    lanes = np.block([[real, imag], [-imag, real]])
    high, low = two_parts(lanes)
    into_lanes = np.concatenate([high, low, high], axis=0)
    high, low = two_parts(lanes.T)
    back_lanes = np.concatenate([high, low, high], axis=0)
    turn = 2.0 * np.pi * np.outer(one + 0.25, one) / LENGTH
    twist = np.stack([np.cos(turn), -np.sin(turn)]).astype(np.float32)
    return into_rows, into_lanes, back_rows, back_lanes, twist


def parts(value):
    high = value.astype(BF16)
    low = (value - high.astype(F32)).astype(BF16)
    return high, low


def dot(left, right, dims=((1,), (0,))):
    return lax.dot_general(left, right, (dims, ((), ())), preferred_element_type=F32)


def forward(pair, into_rows, into_lanes, twist):
    cos, sin = twist[0], twist[1]
    high, low = parts(jnp.concatenate(pair, axis=1))
    step = dot(into_rows[...], jnp.concatenate([high, high, low], axis=0))
    turned = []
    for at in range(len(pair)):
        real = step[:SIDE, at * SIDE : (at + 1) * SIDE]
        imag = step[SIDE:, at * SIDE : (at + 1) * SIDE]
        turned.append(jnp.concatenate([real * cos - imag * sin, real * sin + imag * cos], axis=1))
    high, low = parts(jnp.concatenate(turned, axis=0))
    return dot(jnp.concatenate([high, high, low], axis=1), into_lanes[...])


def backward(spectrum, back_rows, back_lanes, twist):
    cos, sin = twist[0], twist[1]
    count = spectrum.shape[0] // SIDE
    high, low = parts(spectrum)
    step = dot(jnp.concatenate([high, high, low], axis=1), back_lanes[...])
    turned = []
    for at in range(count):
        real = step[at * SIDE : (at + 1) * SIDE, :SIDE]
        imag = step[at * SIDE : (at + 1) * SIDE, SIDE:]
        turned.append(jnp.concatenate([real * cos + imag * sin, imag * cos - real * sin], axis=0))
    high, low = parts(jnp.concatenate(turned, axis=1))
    result = dot(back_rows[...], jnp.concatenate([high, high, low], axis=0))
    return [result[:, at * SIDE : (at + 1) * SIDE] for at in range(count)]


def times(left, right):
    lr, li, rr, ri = left[:, :SIDE], left[:, SIDE:], right[:, :SIDE], right[:, SIDE:]
    return jnp.concatenate([lr * rr - li * ri, lr * ri + li * rr], axis=1)


def times_conj(left, right):
    lr, li, rr, ri = left[:, :SIDE], left[:, SIDE:], right[:, :SIDE], right[:, SIDE:]
    return jnp.concatenate([lr * rr + li * ri, li * rr - lr * ri], axis=1)


def delayed(value, steps):
    row = lax.broadcasted_iota(jnp.int32, value.shape, 0)
    lane = lax.broadcasted_iota(jnp.int32, value.shape, 1)
    turned = pltpu.roll(value, steps, 1)
    above = jnp.where(row == 0, 0.0, pltpu.roll(turned, 1, 0))
    return jnp.where(lane < steps, above, turned)


def advanced(value, steps):
    row = lax.broadcasted_iota(jnp.int32, value.shape, 0)
    lane = lax.broadcasted_iota(jnp.int32, value.shape, 1)
    turned = pltpu.roll(value, SIDE - steps, 1)
    below = jnp.where(row == SIDE - 1, 0.0, pltpu.roll(turned, SIDE - 1, 0))
    return jnp.where(lane >= SIDE - steps, below, turned)


def blocks_kernel(signal, out):
    for at in range(8):
        out[pl.ds(at, 64, stride=8), :] = signal[:, at * SIDE : (at + 1) * SIDE]


def from_blocks(ref):
    return jnp.concatenate([ref[pl.ds(at, 64, stride=8), :] for at in range(8)], axis=1)


def spectrum_kernel(kernel, into_rows, into_lanes, twist, out, rows):
    for at in range(SIDE):
        rows[pl.ds(at, 4, stride=SIDE), :] = kernel[:, at * SIDE : (at + 1) * SIDE]
    for pair in range(2):
        both = [rows[(2 * pair + at) * SIDE : (2 * pair + at + 1) * SIDE, :] for at in range(2)]
        out[pair * 2 * SIDE : (pair + 1) * 2 * SIDE, :] = forward(both, into_rows, into_lanes, twist)


def grad_act_kernel(cot0, cot1, cot2, cot3, mix0, mix1, mix2, mix3, out, mix):
    for at, ref in enumerate((mix0, mix1, mix2, mix3)):
        mix[:, at * 64 : (at + 1) * 64] = ref[...]
    weight_high, weight_low = parts(mix[...])
    weights = jnp.concatenate([weight_high, weight_low, weight_high], axis=1)
    for at in range(8):
        high, low = parts(
            jnp.concatenate([ref[:, at * SIDE : (at + 1) * SIDE] for ref in (cot0, cot1, cot2, cot3)], axis=0)
        )
        out[pl.ds(at, 64, stride=8), :] = dot(weights, jnp.concatenate([high, high, low], axis=0))


def channel(ref, at):
    return ref[:, at * 8 : (at + 1) * 8, :].reshape(SIDE, SIDE)


def tapped(value, gains, at):
    return (
        gains[2, at] * value + gains[1, at] * delayed(value, 1) + gains[0, at] * delayed(value, 2)
    )


def forward_kernel(gains, signal, kernel_spec, into_rows, into_lanes, back_rows, back_lanes, twist, spec, long_conv, act):
    for pair in range(2):
        both = [channel(signal, 2 * pair + at) for at in range(2)]
        place = slice(pair * 2 * SIDE, (pair + 1) * 2 * SIDE)
        spectrum = forward(both, into_rows, into_lanes, twist)
        spec[place, :] = spectrum
        result = backward(times(spectrum, kernel_spec[place, :]), back_rows, back_lanes, twist)
        for at in range(2):
            index = 2 * pair + at
            whole = result[at] + gains[3, index] * both[at]
            long_conv[index] = whole
            value = tapped(whole, gains, index)
            inner = GELU_SCALE * (value + GELU_CUBE * value * value * value)
            active = 0.5 * value * (1.0 + jnp.tanh(inner))
            act[:, index * 8 : (index + 1) * 8, :] = active.reshape(16, 8, SIDE)


def backward_kernel(place_at, gains, grad_act, signal, spec, kernel_spec, long_conv, into_rows, into_lanes, back_rows, back_lanes, twist, grad_in, grad_kernel, small, rows):
    first = 4 * place_at[0]
    line = lax.broadcasted_iota(jnp.int32, (8, SIDE), 0)
    lane = lax.broadcasted_iota(jnp.int32, (8, SIDE), 1)
    sums = jnp.zeros((8, SIDE), F32)
    for pair in range(2):
        place = slice(pair * 2 * SIDE, (pair + 1) * 2 * SIDE)
        grads = []
        for at in range(2):
            index = 2 * pair + at
            whole = long_conv[index]
            later = [delayed(whole, 2), delayed(whole, 1), whole]
            value = sum(gains[tap, index] * later[tap] for tap in range(3))
            square = value * value
            tanh = jnp.tanh(GELU_SCALE * (value + GELU_CUBE * value * square))
            slope = 0.5 * (1.0 + tanh) + 0.5 * value * (1.0 - tanh * tanh) * (
                GELU_SCALE * (1.0 + 3.0 * GELU_CUBE * square)
            )
            grad = channel(grad_act, index) * slope
            for tap in range(3):
                here = (line == tap) & (lane == first + index)
                sums = sums + jnp.where(here, jnp.sum(grad * later[tap]), 0.0)
            grad = (
                gains[2, index] * grad
                + gains[1, index] * advanced(grad, 1)
                + gains[0, index] * advanced(grad, 2)
            )
            here = (line == 3) & (lane == index)
            sums = sums + jnp.where(here, jnp.sum(grad * channel(signal, index)), 0.0)
            grads.append(grad)
        spectrum = forward(grads, into_rows, into_lanes, twist)
        result = backward(times_conj(spectrum, kernel_spec[place, :]), back_rows, back_lanes, twist)
        for at in range(2):
            index = 2 * pair + at
            whole = result[at] + gains[3, index] * grads[at]
            grad_in[:, index * 8 : (index + 1) * 8, :] = whole.reshape(16, 8, SIDE)
        result = backward(times_conj(spectrum, spec[place, :]), back_rows, back_lanes, twist)
        for at in range(2):
            index = 2 * pair + at
            rows[index * SIDE : (index + 1) * SIDE, :] = result[at]
    for at in range(SIDE):
        grad_kernel[:, at * SIDE : (at + 1) * SIDE] = rows[pl.ds(at, 4, stride=SIDE), :]
    small[...] = sums


def grad_mix_kernel(act, cot0, cot1, cot2, cot3, out):
    high, low = parts(from_blocks(act))
    left = jnp.concatenate([high, high, low], axis=1)
    high, low = parts(jnp.concatenate([ref[...] for ref in (cot0, cot1, cot2, cot3)], axis=0))
    result = dot(left, jnp.concatenate([high, low, high], axis=1), ((1,), (1,)))
    for at in range(4):
        out[at, :, :64] = result[:32, at * 64 : (at + 1) * 64]
        out[at, :, 64:] = result[32:, at * 64 : (at + 1) * 64]


def outputs_kernel(place_at, signal, act0, act1, act2, act3, mix, out):
    me = place_at[1]
    high, low = parts(
        jnp.concatenate(
            [mix[pl.ds(pl.multiple_of(64 * jnp.bitwise_xor(me, at), 64), 64), :] for at in range(4)], axis=0
        )
    )
    weights = jnp.concatenate([high, low, high], axis=0)
    for at in range(8):
        high, low = parts(
            jnp.concatenate([ref[pl.ds(at, 64, stride=8), :] for ref in (act0, act1, act2, act3)], axis=0)
        )
        mixed = dot(weights, jnp.concatenate([high, high, low], axis=0), ((0,), (0,)))
        lanes = slice(at * SIDE, (at + 1) * SIDE)
        out[:, lanes] = signal[:, lanes] + mixed


def grad_inputs_kernel(cotangent, grad_in, out):
    for at in range(8):
        lanes = slice(at * SIDE, (at + 1) * SIDE)
        out[:, lanes] = cotangent[:, lanes] + grad_in[pl.ds(at, 64, stride=8), :]


def final_kernel(place_at, total0, total1, total2, total3, out):
    me = place_at[1]
    for at in range(4):
        whole = total0[at] + total1[at] + total2[at] + total3[at]
        start = pl.multiple_of(64 * jnp.bitwise_xor(me, at), 64)
        out[pl.ds(start, 32), :] = whole[:, :64]
        out[pl.ds(start + 32, 32), :] = whole[:, 64:]


def call(kernel, outs, *args, scalars=0, scratch=()):
    shapes = [jax.ShapeDtypeStruct(shape, F32) for shape in outs]
    return pl.pallas_call(
        kernel,
        out_shape=shapes if len(shapes) > 1 else shapes[0],
        in_specs=[SMEM] * scalars + [VMEM] * (len(args) - scalars),
        out_specs=[VMEM] * len(shapes) if len(shapes) > 1 else VMEM,
        scratch_shapes=[pltpu.VMEM(shape, F32) for shape in scratch],
        compiler_params=pltpu.CompilerParams(vmem_limit_bytes=48 * 1024 * 1024),
        name=kernel.__name__,
    )(*args)


def swapped(value, axes, flip):
    count = lax.axis_size(axes)
    return lax.ppermute(value, axes, [(at, at ^ flip) for at in range(count)])


def turned(value):
    return lax.all_to_all(value.reshape(16, 32, SIDE), "seq", 0, 0, tiled=True)


def shards(inputs, cotangent, conv_weight, kernel, skip_gain, mix_weight):
    signal = inputs[0]
    grad_out = cotangent[0]
    seq, chan = lax.axis_index("seq"), lax.axis_index("chan")
    place_at = jnp.stack([seq, chan]).astype(jnp.int32)
    gains = jnp.concatenate([lax.dynamic_slice(conv_weight, (0, 4 * seq), (3, 4)), skip_gain[None]], axis=0)
    into_rows, into_lanes, back_rows, back_lanes, twist = (jnp.asarray(table) for table in tables())

    signal_in = turned(call(blocks_kernel, [(512, SIDE)], signal))

    cot2 = swapped(grad_out, "chan", 2)
    cot1 = swapped(grad_out, "chan", 1)
    cot3 = swapped(cot2, "chan", 1)
    cots = (grad_out, cot1, cot2, cot3)
    mixes = []
    for flip in range(4):
        block = lax.dynamic_slice(mix_weight, (64 * jnp.bitwise_xor(chan, flip), 0), (64, 64))
        mixes.append(swapped(block, "chan", flip) if flip else block)
    grad_act = turned(call(grad_act_kernel, [(512, SIDE)], *cots, *mixes, scratch=[(64, 256)]))

    kernel_spec = call(
        spectrum_kernel, [(512, 256)], kernel, into_rows, into_lanes, twist, scratch=[(512, SIDE)]
    )
    spec, long_conv, act = call(
        forward_kernel,
        [(512, 256), (4, SIDE, SIDE), (16, 32, SIDE)],
        gains, signal_in, kernel_spec, into_rows, into_lanes, back_rows, back_lanes, twist,
        scalars=1,
    )
    act0 = turned(act).reshape(512, SIDE)
    grad_in, kernel_local, small = call(
        backward_kernel,
        [(16, 32, SIDE), (4, LENGTH), (8, SIDE)],
        place_at, gains, grad_act, signal_in, spec, kernel_spec, long_conv,
        into_rows, into_lanes, back_rows, back_lanes, twist,
        scalars=2, scratch=[(512, SIDE)],
    )
    grad_mixes = call(grad_mix_kernel, [(4, 32, SIDE)], act0, *cots)
    act2 = swapped(act0, "chan", 2)
    act1 = swapped(act0, "chan", 1)
    act3 = swapped(act2, "chan", 1)
    grad_conv_long = turned(grad_in).reshape(512, SIDE)

    grad_kernel = kernel_local + swapped(kernel_local, "dp", 1)
    sums = small + swapped(small, "dp", 1)
    grad_skip = sums[3, :4]

    blocks = [
        sum(swapped(grad_mixes[at], ("dp", "chan"), 4 * far + at) if far or at else grad_mixes[at] for far in range(2))
        for at in range(4)
    ]
    total = jnp.concatenate([jnp.stack(blocks), jnp.pad(sums, ((0, 24), (0, 0)))[None]], axis=0)
    total = total + swapped(total, "seq", 4) + swapped(total, "seq", 8) + swapped(total, "seq", 12)
    totals = [total] + [swapped(total, "seq", at) for at in (1, 2, 3)]
    grad_mix = call(final_kernel, [(256, 64)], place_at, *totals, scalars=1)
    grad_conv = sum(one[4, :3, :64] for one in totals)

    outputs = call(outputs_kernel, [(64, 1024)], place_at, signal, act0, act1, act2, act3, mix_weight, scalars=1)
    grad_inputs = call(grad_inputs_kernel, [(64, 1024)], grad_out, grad_conv_long)
    return (outputs[None], grad_inputs[None], grad_kernel, grad_skip, grad_mix, grad_conv)


def solution(mesh):
    placed = (
        P("dp", "chan", "seq"),
        P("dp", "chan", "seq"),
        P(None, "chan"),
        P(("chan", "seq"), None),
        P(("chan", "seq")),
        P(None, "chan"),
    )
    return jax.shard_map(
        shards,
        mesh=mesh,
        in_specs=placed,
        out_specs=(
            P("dp", "chan", "seq"),
            P("dp", "chan", "seq"),
            P(("chan", "seq"), None),
            P(("chan", "seq")),
            P(None, "chan"),
            P(None, "chan"),
        ),
        check_vma=False,
    )
```

```python
import functools
import math

import jax
import jax.numpy as jnp
import ml_dtypes
import numpy as np
from jax import lax
from jax.experimental import pallas as pl
from jax.experimental.pallas import tpu as pltpu
from jax.sharding import PartitionSpec as P

SIDE = 128
LENGTH = SIDE * SIDE
F32 = jnp.float32
BF16 = jnp.bfloat16
GELU_SCALE = math.sqrt(2.0 / math.pi)
GELU_CUBE = 0.044715
VMEM = pl.BlockSpec(memory_space=pltpu.VMEM)
SMEM = pl.BlockSpec(memory_space=pltpu.SMEM)
HBM = pl.BlockSpec(memory_space=pltpu.HBM)


def two_parts(table):
    high = table.astype(ml_dtypes.bfloat16)
    low = (table - high.astype(np.float64)).astype(ml_dtypes.bfloat16)
    return high, low


@functools.cache
def tables():
    one = np.arange(SIDE, dtype=np.float64)
    turn = 2.0 * np.pi * np.outer(one + 0.25, one) / SIDE
    rows = np.concatenate([np.cos(turn), -np.sin(turn)], axis=0)
    high, low = two_parts(rows)
    into_rows = np.concatenate([high, low, high], axis=1)
    high, low = two_parts(rows.T / LENGTH)
    back_rows = np.concatenate([high, low, high], axis=1)
    turn = 2.0 * np.pi * np.outer(one, one) / SIDE
    real, imag = np.cos(turn), -np.sin(turn)
    lanes = np.block([[real, imag], [-imag, real]])
    high, low = two_parts(lanes)
    into_lanes = np.concatenate([high, low, high], axis=0)
    high, low = two_parts(lanes.T)
    back_lanes = np.concatenate([high, low, high], axis=0)
    turn = 2.0 * np.pi * np.outer(one + 0.25, one) / LENGTH
    twist = np.stack([np.cos(turn), -np.sin(turn)]).astype(np.float32)
    return into_rows, into_lanes, back_rows, back_lanes, twist


def parts(value):
    high = value.astype(BF16)
    low = (value - high.astype(F32)).astype(BF16)
    return high, low


def dot(left, right, dims=((1,), (0,))):
    return lax.dot_general(left, right, (dims, ((), ())), preferred_element_type=F32)


def forward(pair, into_rows, into_lanes, twist):
    cos, sin = twist[0], twist[1]
    high, low = parts(jnp.concatenate(pair, axis=1))
    step = dot(into_rows[...], jnp.concatenate([high, high, low], axis=0))
    turned = []
    for at in range(len(pair)):
        real = step[:SIDE, at * SIDE : (at + 1) * SIDE]
        imag = step[SIDE:, at * SIDE : (at + 1) * SIDE]
        turned.append(jnp.concatenate([real * cos - imag * sin, real * sin + imag * cos], axis=1))
    high, low = parts(jnp.concatenate(turned, axis=0))
    return dot(jnp.concatenate([high, high, low], axis=1), into_lanes[...])


def backward(spectrum, back_rows, back_lanes, twist):
    cos, sin = twist[0], twist[1]
    count = spectrum.shape[0] // SIDE
    high, low = parts(spectrum)
    step = dot(jnp.concatenate([high, high, low], axis=1), back_lanes[...])
    turned = []
    for at in range(count):
        real = step[at * SIDE : (at + 1) * SIDE, :SIDE]
        imag = step[at * SIDE : (at + 1) * SIDE, SIDE:]
        turned.append(jnp.concatenate([real * cos + imag * sin, imag * cos - real * sin], axis=0))
    high, low = parts(jnp.concatenate(turned, axis=1))
    result = dot(back_rows[...], jnp.concatenate([high, high, low], axis=0))
    return [result[:, at * SIDE : (at + 1) * SIDE] for at in range(count)]


def times(left, right):
    lr, li, rr, ri = left[:, :SIDE], left[:, SIDE:], right[:, :SIDE], right[:, SIDE:]
    return jnp.concatenate([lr * rr - li * ri, lr * ri + li * rr], axis=1)


def times_conj(left, right):
    lr, li, rr, ri = left[:, :SIDE], left[:, SIDE:], right[:, :SIDE], right[:, SIDE:]
    return jnp.concatenate([lr * rr + li * ri, li * rr - lr * ri], axis=1)


def delayed(value, steps):
    row = lax.broadcasted_iota(jnp.int32, value.shape, 0)
    lane = lax.broadcasted_iota(jnp.int32, value.shape, 1)
    turned = pltpu.roll(value, steps, 1)
    above = jnp.where(row == 0, 0.0, pltpu.roll(turned, 1, 0))
    return jnp.where(lane < steps, above, turned)


def advanced(value, steps):
    row = lax.broadcasted_iota(jnp.int32, value.shape, 0)
    lane = lax.broadcasted_iota(jnp.int32, value.shape, 1)
    turned = pltpu.roll(value, SIDE - steps, 1)
    below = jnp.where(row == SIDE - 1, 0.0, pltpu.roll(turned, SIDE - 1, 0))
    return jnp.where(lane >= SIDE - steps, below, turned)


def blocks_kernel(signal, out):
    for at in range(8):
        out[pl.ds(at, 64, stride=8), :] = signal[:, at * SIDE : (at + 1) * SIDE]


def from_blocks(ref):
    return jnp.concatenate([ref[pl.ds(at, 64, stride=8), :] for at in range(8)], axis=1)


def spectrum_kernel(kernel, into_rows, into_lanes, twist, out, rows):
    for at in range(SIDE):
        rows[pl.ds(at, 4, stride=SIDE), :] = kernel[:, at * SIDE : (at + 1) * SIDE]
    for pair in range(2):
        both = [rows[(2 * pair + at) * SIDE : (2 * pair + at + 1) * SIDE, :] for at in range(2)]
        out[pair * 2 * SIDE : (pair + 1) * 2 * SIDE, :] = forward(both, into_rows, into_lanes, twist)


def mix_pair(place_at, mix, mix_far):
    chan = place_at[1]
    start = pl.multiple_of(128 * lax.shift_right_logical(chan, 1), 128)
    both = jnp.concatenate([mix[:, pl.ds(start, 128)], mix_far[...]], axis=0)
    return pltpu.roll(both, 64 * jnp.bitwise_and(chan, 1), 1)


def grad_act_kernel(place_at, cot, cot_far, mix, mix_far, own, other):
    weight_high, weight_low = parts(mix_pair(place_at, mix, mix_far).T)
    weights = jnp.concatenate([weight_high, weight_low, weight_high], axis=1)
    for at in range(8):
        lanes = slice(at * SIDE, (at + 1) * SIDE)
        high, low = parts(jnp.concatenate([cot[:, lanes], cot_far[:, lanes]], axis=0))
        result = dot(weights, jnp.concatenate([high, high, low], axis=0))
        own[pl.ds(at, 64, stride=8), :] = result[:64]
        other[pl.ds(at, 64, stride=8), :] = result[64:]


def channel(ref, at):
    return ref[:, at * 8 : (at + 1) * 8, :].reshape(SIDE, SIDE)


def gains_of(place_at, taps, at):
    index = 4 * place_at[0] + at
    return taps[0, index], taps[1, index], taps[2, index]


def moved(copies):
    for one in copies:
        one.start()
    return copies


def forward_kernel(
    place_at, taps, skip, signal, kernel_spec, into_rows, into_lanes, back_rows, back_lanes, twist,
    spec, long_conv, act_out, act, sems,
):
    copies = []
    for pair in range(2):
        both = [channel(signal, 2 * pair + at) for at in range(2)]
        place = slice(pair * 2 * SIDE, (pair + 1) * 2 * SIDE)
        spectrum = forward(both, into_rows, into_lanes, twist)
        spec[place, :] = spectrum
        result = backward(times(spectrum, kernel_spec[place, :]), back_rows, back_lanes, twist)
        for at in range(2):
            index = 2 * pair + at
            gains = gains_of(place_at, taps, index)
            whole = result[at] + skip[index] * both[at]
            long_conv[index] = whole
            value = gains[2] * whole + gains[1] * delayed(whole, 1) + gains[0] * delayed(whole, 2)
            inner = GELU_SCALE * (value + GELU_CUBE * value * value * value)
            active = 0.5 * value * (1.0 + jnp.tanh(inner))
            act[:, index * 8 : (index + 1) * 8, :] = active.reshape(16, 8, SIDE)
        rows = pl.ds(pair * 16, 16)
        copies += moved([pltpu.make_async_copy(act.at[:, rows, :], act_out.at[:, rows, :], sems.at[pair])])
    for one in copies:
        one.wait()


def join_kernel(act, own, near, out, total, sem):
    total[...] = (own[...] + near[...]).reshape(16, 32, SIDE)
    copy = pltpu.make_async_copy(total, out.at[:, pl.ds(32, 32), :], sem)
    copy.start()
    copy.wait()


def slope_kernel(place_at, taps, grad_act, signal, long_conv, grads, small):
    first = 4 * place_at[0]
    line = lax.broadcasted_iota(jnp.int32, (8, SIDE), 0)
    lane = lax.broadcasted_iota(jnp.int32, (8, SIDE), 1)
    sums = jnp.zeros((8, SIDE), F32)
    for index in range(4):
        gains = gains_of(place_at, taps, index)
        whole = long_conv[index]
        later = [delayed(whole, 2), delayed(whole, 1), whole]
        value = gains[2] * whole + gains[1] * later[1] + gains[0] * later[0]
        square = value * value
        tanh = jnp.tanh(GELU_SCALE * (value + GELU_CUBE * value * square))
        slope = 0.5 * (1.0 + tanh) + 0.5 * value * (1.0 - tanh * tanh) * (
            GELU_SCALE * (1.0 + 3.0 * GELU_CUBE * square)
        )
        grad = channel(grad_act, 4 + index) * slope
        for tap in range(3):
            here = (line == tap) & (lane == first + index)
            sums = sums + jnp.where(here, jnp.sum(grad * later[tap]), 0.0)
        grad = gains[2] * grad + gains[1] * advanced(grad, 1) + gains[0] * advanced(grad, 2)
        here = (line == 3) & (lane == index)
        sums = sums + jnp.where(here, jnp.sum(grad * channel(signal, index)), 0.0)
        grads[index] = grad
    small[...] = sums


def backward_kernel(
    skip, grads, spec, kernel_spec, into_rows, into_lanes, back_rows, back_lanes, twist,
    grad_out, kernel_out, grad_in, rows, sems,
):
    copies = []
    for pair in range(2):
        place = slice(pair * 2 * SIDE, (pair + 1) * 2 * SIDE)
        both = [grads[2 * pair + at] for at in range(2)]
        spectrum = forward(both, into_rows, into_lanes, twist)
        result = backward(times_conj(spectrum, kernel_spec[place, :]), back_rows, back_lanes, twist)
        for at in range(2):
            index = 2 * pair + at
            whole = result[at] + skip[index] * both[at]
            grad_in[:, index * 8 : (index + 1) * 8, :] = whole.reshape(16, 8, SIDE)
        lines = pl.ds(pair * 16, 16)
        copies += moved([pltpu.make_async_copy(grad_in.at[:, lines, :], grad_out.at[:, lines, :], sems.at[pair])])
        result = backward(times_conj(spectrum, spec[place, :]), back_rows, back_lanes, twist)
        for at in range(2):
            index = 2 * pair + at
            rows[index * SIDE : (index + 1) * SIDE, :] = result[at]
    for at in range(SIDE):
        kernel_out[:, at * SIDE : (at + 1) * SIDE] = rows[pl.ds(at, 4, stride=SIDE), :]
    for one in copies:
        one.wait()


def tail_kernel(place_at, act, act_near, cot, cot_far, signal, mix, mix_far, small, mine, theirs, out, out_far):
    active = jnp.concatenate([from_blocks(act), from_blocks(act_near)], axis=0)
    act_high, act_low = parts(active)
    high, low = parts(jnp.concatenate([cot[...], cot_far[...]], axis=0))
    result = dot(
        jnp.concatenate([high, low, high], axis=1),
        jnp.concatenate([act_high, act_high, act_low], axis=1),
        ((1,), (1,)),
    )
    mine[:64, :] = result[:64]
    mine[64:, :] = small[...]
    theirs[...] = result[64:]
    high, low = parts(mix_pair(place_at, mix, mix_far))
    mixed = dot(
        jnp.concatenate([high, low, high], axis=1),
        jnp.concatenate([act_high, act_high, act_low], axis=0),
    )
    out[...] = signal[...] + mixed[:64]
    out_far[...] = mixed[64:]


def merge_kernel(mine, mine_far, theirs, theirs_far, out):
    out[:64, :] = mine[:64, :] + mine_far[:64, :]
    out[64:128, :] = theirs[...] + theirs_far[...]
    out[128:, :] = mine[64:, :] + mine_far[64:, :]


def grad_inputs_kernel(cotangent, grad_in, out):
    for at in range(8):
        lanes = slice(at * SIDE, (at + 1) * SIDE)
        out[:, lanes] = cotangent[:, lanes] + grad_in[pl.ds(at, 64, stride=8), :]


def final_kernel(place_at, total0, total1, total2, total3, out, taps):
    chan = place_at[1]
    whole = total0[...] + total1[...] + total2[...] + total3[...]
    turn = 64 * jnp.bitwise_and(chan, 1)
    start = 128 * lax.shift_right_logical(chan, 1)
    out[:, pl.ds(pl.multiple_of(start, 128), 128)] = pltpu.roll(whole[:64], turn, 1)
    out[:, pl.ds(pl.multiple_of(128 - start, 128), 128)] = pltpu.roll(whole[64:128], turn, 1)
    taps[...] = whole[128:131, :64]


def call(kernel, outs, *args, scalars=0, far=(), far_outs=(), scratch=(), after=(), aliases=()):
    shapes = [jax.ShapeDtypeStruct(shape, F32) for shape in outs]
    count = len(args)

    def body(*refs):
        kernel(*refs[:count], *refs[count + len(after) :])

    ins = [SMEM if at < scalars else HBM if at in far else VMEM for at in range(count)]
    places = [HBM if at in far_outs else VMEM for at in range(len(outs))]
    return pl.pallas_call(
        body,
        out_shape=shapes if len(shapes) > 1 else shapes[0],
        in_specs=ins + [pl.BlockSpec(memory_space=pl.ANY)] * len(after),
        out_specs=places if len(shapes) > 1 else places[0],
        scratch_shapes=[shape if not isinstance(shape, tuple) else pltpu.VMEM(shape, F32) for shape in scratch],
        compiler_params=pltpu.CompilerParams(vmem_limit_bytes=20 * 1024 * 1024),
        input_output_aliases=dict(aliases),
        name=kernel.__name__,
    )(*args, *after)


def swapped(value, axes, flip):
    count = lax.axis_size(axes)
    return lax.ppermute(value, axes, [(at, at ^ flip) for at in range(count)])


def turned(value):
    return lax.all_to_all(value, "seq", 0, 0, tiled=True)


def shards(inputs, cotangent, conv_weight, kernel, skip_gain, mix_weight):
    signal = inputs[0]
    grad_out = cotangent[0]
    seq, chan = lax.axis_index("seq"), lax.axis_index("chan")
    place_at = jnp.stack([seq, chan]).astype(jnp.int32)
    into_rows, into_lanes, back_rows, back_lanes, twist = (jnp.asarray(table) for table in tables())
    mix = mix_weight.T

    cot_far = swapped(grad_out, "chan", 2)
    far = jnp.bitwise_xor(lax.shift_right_logical(chan, 1), 1)
    mix_far = swapped(lax.dynamic_slice(mix, (0, 128 * far), (64, 128)), "chan", 2)
    signal_blocks = call(blocks_kernel, [(512, SIDE)], signal)
    signal_in = turned(signal_blocks.reshape(16, 32, SIDE))
    kernel_spec = call(
        spectrum_kernel, [(512, 256)], kernel, into_rows, into_lanes, twist,
        scratch=[(512, SIDE)], after=[signal_blocks],
    )
    grad_own, grad_other = call(
        grad_act_kernel, [(512, SIDE)] * 2, place_at, grad_out, cot_far, mix, mix_far,
        scalars=1, after=[kernel_spec, signal_in],
    )
    grad_near = swapped(grad_other, "chan", 1)
    spec, long_conv, act = call(
        forward_kernel,
        [(512, 256), (4, SIDE, SIDE), (16, 64, SIDE)],
        place_at, conv_weight, skip_gain, signal_in, kernel_spec,
        into_rows, into_lanes, back_rows, back_lanes, twist,
        scalars=3, far_outs=(2,), after=[grad_own],
        scratch=[(16, 32, SIDE), pltpu.SemaphoreType.DMA((2,))],
    )
    act = call(
        join_kernel, [(16, 64, SIDE)], act, grad_own, grad_near,
        far=(0,), far_outs=(0,), aliases={0: 0}, scratch=[(16, 32, SIDE), pltpu.SemaphoreType.DMA],
    )
    act_in = turned(act)
    act_own = act_in[:, :32].reshape(512, SIDE)
    act_near = swapped(act_own, "chan", 1)
    grads, small = call(
        slope_kernel, [(4, SIDE, SIDE), (8, SIDE)], place_at, conv_weight, act_in, signal_in, long_conv, scalars=2
    )
    mine, theirs, out_own, out_far = call(
        tail_kernel,
        [(72, SIDE), (64, SIDE), (64, 1024), (64, 1024)],
        place_at, act_own, act_near, grad_out, cot_far, signal, mix, mix_far, small,
        scalars=1,
    )
    grad_long, kernel_local = call(
        backward_kernel,
        [(16, 32, SIDE), (4, LENGTH)],
        skip_gain, grads, spec, kernel_spec, into_rows, into_lanes, back_rows, back_lanes, twist,
        scalars=1, far_outs=(0,), after=[mine],
        scratch=[(16, 32, SIDE), (512, SIDE), pltpu.SemaphoreType.DMA((2,))],
    )
    both = ("dp", "chan")
    total = call(
        merge_kernel, [(136, SIDE)], mine, swapped(mine, both, 4), swapped(theirs, both, 2), swapped(theirs, both, 6),
        after=[kernel_local],
    )
    grad_skip = total[131, :4]
    outputs = out_own + swapped(out_far, "chan", 2)
    grad_in = turned(grad_long).reshape(512, SIDE)
    grad_inputs = call(grad_inputs_kernel, [(64, 1024)], grad_out, grad_in)
    grad_kernel = kernel_local + swapped(kernel_local, "dp", 1)
    total = total + swapped(total, "seq", 4) + swapped(total, "seq", 8) + swapped(total, "seq", 12)
    grad_mix, grad_conv = call(
        final_kernel, [(64, 256), (3, 64)], place_at, total, *(swapped(total, "seq", at) for at in (1, 2, 3)),
        scalars=1, after=[grad_inputs, grad_kernel, outputs],
    )
    return (outputs[None], grad_inputs[None], grad_kernel, grad_skip, grad_mix.T, grad_conv)


def solution(mesh):
    placed = (
        P("dp", "chan", "seq"),
        P("dp", "chan", "seq"),
        P(None, "chan"),
        P(("chan", "seq"), None),
        P(("chan", "seq")),
        P(None, "chan"),
    )
    return jax.shard_map(
        shards,
        mesh=mesh,
        in_specs=placed,
        out_specs=(
            P("dp", "chan", "seq"),
            P("dp", "chan", "seq"),
            P(("chan", "seq"), None),
            P(("chan", "seq")),
            P(None, "chan"),
            P(None, "chan"),
        ),
        check_vma=False,
    )
```

```python
import functools
import math

import jax
import jax.numpy as jnp
import ml_dtypes
import numpy as np
from jax import lax
from jax.experimental import pallas as pl
from jax.experimental.pallas import tpu as pltpu
from jax.sharding import PartitionSpec as P

SIDE = 128
LENGTH = SIDE * SIDE
F32 = jnp.float32
BF16 = jnp.bfloat16
GELU_SCALE = math.sqrt(2.0 / math.pi)
GELU_CUBE = 0.044715
VMEM = pl.BlockSpec(memory_space=pltpu.VMEM)
SMEM = pl.BlockSpec(memory_space=pltpu.SMEM)
HBM = pl.BlockSpec(memory_space=pltpu.HBM)


def two_parts(table):
    high = table.astype(ml_dtypes.bfloat16)
    low = (table - high.astype(np.float64)).astype(ml_dtypes.bfloat16)
    return high, low


@functools.cache
def tables():
    one = np.arange(SIDE, dtype=np.float64)
    turn = 2.0 * np.pi * np.outer(one + 0.25, one) / SIDE
    rows = np.concatenate([np.cos(turn), -np.sin(turn)], axis=0)
    high, low = two_parts(rows)
    into_rows = np.concatenate([high, low, high], axis=1)
    high, low = two_parts(rows.T / LENGTH)
    back_rows = np.concatenate([high, low, high], axis=1)
    turn = 2.0 * np.pi * np.outer(one, one) / SIDE
    real, imag = np.cos(turn), -np.sin(turn)
    lanes = np.block([[real, imag], [-imag, real]])
    high, low = two_parts(lanes)
    into_lanes = np.concatenate([high, low, high], axis=0)
    high, low = two_parts(lanes.T)
    back_lanes = np.concatenate([high, low, high], axis=0)
    turn = 2.0 * np.pi * np.outer(one + 0.25, one) / LENGTH
    twist = np.stack([np.cos(turn), -np.sin(turn)]).astype(np.float32)
    return into_rows, into_lanes, back_rows, back_lanes, twist


def parts(value):
    high = value.astype(BF16)
    low = (value - high.astype(F32)).astype(BF16)
    return high, low


def dot(left, right, dims=((1,), (0,))):
    return lax.dot_general(left, right, (dims, ((), ())), preferred_element_type=F32)


def forward(pair, into_rows, into_lanes, twist):
    cos, sin = twist[0], twist[1]
    high, low = parts(jnp.concatenate(pair, axis=1))
    step = dot(into_rows[...], jnp.concatenate([high, high, low], axis=0))
    turned = []
    for at in range(len(pair)):
        real = step[:SIDE, at * SIDE : (at + 1) * SIDE]
        imag = step[SIDE:, at * SIDE : (at + 1) * SIDE]
        turned.append(jnp.concatenate([real * cos - imag * sin, real * sin + imag * cos], axis=1))
    high, low = parts(jnp.concatenate(turned, axis=0))
    return dot(jnp.concatenate([high, high, low], axis=1), into_lanes[...])


def backward(spectrum, back_rows, back_lanes, twist):
    cos, sin = twist[0], twist[1]
    count = spectrum.shape[0] // SIDE
    high, low = parts(spectrum)
    step = dot(jnp.concatenate([high, high, low], axis=1), back_lanes[...])
    turned = []
    for at in range(count):
        real = step[at * SIDE : (at + 1) * SIDE, :SIDE]
        imag = step[at * SIDE : (at + 1) * SIDE, SIDE:]
        turned.append(jnp.concatenate([real * cos + imag * sin, imag * cos - real * sin], axis=0))
    high, low = parts(jnp.concatenate(turned, axis=1))
    result = dot(back_rows[...], jnp.concatenate([high, high, low], axis=0))
    return [result[:, at * SIDE : (at + 1) * SIDE] for at in range(count)]


def times(left, right):
    lr, li, rr, ri = left[:, :SIDE], left[:, SIDE:], right[:, :SIDE], right[:, SIDE:]
    return jnp.concatenate([lr * rr - li * ri, lr * ri + li * rr], axis=1)


def times_conj(left, right):
    lr, li, rr, ri = left[:, :SIDE], left[:, SIDE:], right[:, :SIDE], right[:, SIDE:]
    return jnp.concatenate([lr * rr + li * ri, li * rr - lr * ri], axis=1)


def delayed(value, steps):
    row = lax.broadcasted_iota(jnp.int32, value.shape, 0)
    lane = lax.broadcasted_iota(jnp.int32, value.shape, 1)
    turned = pltpu.roll(value, steps, 1)
    above = jnp.where(row == 0, 0.0, pltpu.roll(turned, 1, 0))
    return jnp.where(lane < steps, above, turned)


def advanced(value, steps):
    row = lax.broadcasted_iota(jnp.int32, value.shape, 0)
    lane = lax.broadcasted_iota(jnp.int32, value.shape, 1)
    turned = pltpu.roll(value, SIDE - steps, 1)
    below = jnp.where(row == SIDE - 1, 0.0, pltpu.roll(turned, SIDE - 1, 0))
    return jnp.where(lane >= SIDE - steps, below, turned)


def blocks_kernel(signal, out):
    for at in range(8):
        out[pl.ds(at, 64, stride=8), :] = signal[:, at * SIDE : (at + 1) * SIDE]


def from_blocks(ref):
    return jnp.concatenate([ref[pl.ds(at, 64, stride=8), :] for at in range(8)], axis=1)


def spectrum_kernel(place_at, taps, skip, kernel, into_rows, into_lanes, twist, out, gains, rows):
    for at in range(SIDE):
        rows[pl.ds(at, 4, stride=SIDE), :] = kernel[:, at * SIDE : (at + 1) * SIDE]
    line = lax.broadcasted_iota(jnp.int32, (SIDE, SIDE), 0)
    lane = lax.broadcasted_iota(jnp.int32, (SIDE, SIDE), 1)
    start = (line == 0) & (lane == 0)
    every = [
        rows[at * SIDE : (at + 1) * SIDE, :] + jnp.where(start, skip[at], 0.0) for at in range(4)
    ]
    out[...] = forward(every, into_rows, into_lanes, twist)
    line, lane = line[:16], lane[:16]
    first, chan = 4 * place_at[0], place_at[1]
    result = jnp.where(line == 3, jnp.bitwise_and(chan, 1).astype(F32), 0.0)
    result = jnp.where(line == 4, lax.shift_right_logical(chan, 1).astype(F32), result)
    result = jnp.where((line >= 8) & (line < 12) & (lane == first + line - 8), 1.0, result)
    for tap in range(3):
        for at in range(4):
            result = jnp.where((line == tap) & (lane == at), taps[tap, first + at], result)
    gains[...] = result


def weights_kernel(place_at, mix, mix_far, _rows, _lanes, into, back):
    chan = place_at[1]
    start = pl.multiple_of(128 * lax.shift_right_logical(chan, 1), 128)
    both = jnp.concatenate([mix[:, pl.ds(start, 128)], mix_far[...]], axis=0)
    both = pltpu.roll(both, 64 * jnp.bitwise_and(chan, 1), 1)
    high, low = parts(both)
    back[...] = jnp.concatenate([high, low, high], axis=1)
    high, low = parts(both.T)
    into[...] = jnp.concatenate([high, low, high], axis=1)


def grad_act_kernel(cot, cot_far, weights, own, other):
    for half in range(4):
        lanes = slice(half * 256, (half + 1) * 256)
        high, low = parts(jnp.concatenate([cot[:, lanes], cot_far[:, lanes]], axis=0))
        result = dot(weights[...], jnp.concatenate([high, high, low], axis=0))
        for at in range(2):
            place = pl.ds(2 * half + at, 64, stride=8)
            own[place, :] = result[:64, at * SIDE : (at + 1) * SIDE]
            other[place, :] = result[64:, at * SIDE : (at + 1) * SIDE]


def channel(ref, at):
    return ref[:, at * 8 : (at + 1) * 8, :].reshape(SIDE, SIDE)


def gains_of(gains, at):
    return [jnp.broadcast_to(gains[tap : tap + 1, at : at + 1], (SIDE, SIDE)) for tap in range(3)]


def moved(copies):
    for one in copies:
        one.start()
    return copies


def forward_kernel(
    gains, signal, kernel_spec, into_rows, into_lanes, back_rows, back_lanes, twist,
    spec, long_conv, slopes, act_out, act, sem,
):
    spectrum = forward([channel(signal, at) for at in range(4)], into_rows, into_lanes, twist)
    spec[...] = spectrum
    result = backward(times(spectrum, kernel_spec[...]), back_rows, back_lanes, twist)
    for index in range(4):
        taps = gains_of(gains, index)
        whole = result[index]
        long_conv[index] = whole
        value = taps[2] * whole + taps[1] * delayed(whole, 1) + taps[0] * delayed(whole, 2)
        square = value * value
        half = 0.5 + 0.5 * jnp.tanh(value * (GELU_SCALE + GELU_SCALE * GELU_CUBE * square))
        act[:, index * 8 : (index + 1) * 8, :] = (value * half).reshape(16, 8, SIDE)
        slopes[index] = half + half * (1.0 - half) * value * (
            2.0 * GELU_SCALE + 6.0 * GELU_SCALE * GELU_CUBE * square
        )
    copy = pltpu.make_async_copy(act, act_out.at[:, pl.ds(0, 32), :], sem)
    copy.start()
    copy.wait()


def join_kernel(act, own, near, out, total, sem):
    total[...] = (own[...] + near[...]).reshape(16, 32, SIDE)
    copy = pltpu.make_async_copy(total, out.at[:, pl.ds(32, 32), :], sem)
    copy.start()
    copy.wait()


def slope_kernel(gains, grad_act, signal, long_conv, slopes, grads, small):
    small[...] = jnp.zeros_like(small)
    for index in range(4):
        taps = gains_of(gains, index)
        grad = channel(grad_act, 4 + index) * slopes[index]
        later = [advanced(grad, 2), advanced(grad, 1), grad]
        grads[index] = taps[0] * later[0] + taps[1] * later[1] + taps[2] * later[2]
        pairs = [one * long_conv[index] for one in later] + [grads[index] * channel(signal, index)]
        sums = jnp.concatenate([jnp.sum(one, axis=0, keepdims=True) for one in pairs], axis=0)
        small[:4, :] = small[:4, :] + jnp.sum(sums, axis=1, keepdims=True) * gains[8 + index : 9 + index, :]


def backward_kernel(
    grads, spec, kernel_spec, into_rows, into_lanes, back_rows, back_lanes, twist,
    grad_out, kernel_out, grad_in, rows, sem,
):
    spectrum = forward([grads[at] for at in range(4)], into_rows, into_lanes, twist)
    result = backward(times_conj(spectrum, kernel_spec[...]), back_rows, back_lanes, twist)
    for at in range(4):
        grad_in[:, at * 8 : (at + 1) * 8, :] = result[at].reshape(16, 8, SIDE)
    copy = pltpu.make_async_copy(grad_in, grad_out, sem)
    copy.start()
    result = backward(times_conj(spectrum, spec[...]), back_rows, back_lanes, twist)
    for at in range(4):
        rows[at * SIDE : (at + 1) * SIDE, :] = result[at]
    for at in range(SIDE):
        kernel_out[:, at * SIDE : (at + 1) * SIDE] = rows[pl.ds(at, 4, stride=SIDE), :]
    copy.wait()


def tail_kernel(act, act_near, cot, cot_far, signal, weights, small, mine, theirs, out, out_far):
    active = jnp.concatenate([from_blocks(act), from_blocks(act_near)], axis=0)
    act_high, act_low = parts(active)
    high, low = parts(jnp.concatenate([cot[...], cot_far[...]], axis=0))
    result = dot(
        jnp.concatenate([high, low, high], axis=1),
        jnp.concatenate([act_high, act_high, act_low], axis=1),
        ((1,), (1,)),
    )
    mine[:64, :] = result[:64]
    mine[64:, :] = small[...]
    theirs[...] = result[64:]
    mixed = dot(weights[...], jnp.concatenate([act_high, act_high, act_low], axis=0))
    out[...] = signal[...] + mixed[:64]
    out_far[...] = mixed[64:]


def merge_kernel(mine, mine_far, theirs, theirs_far, out):
    out[:64, :] = mine[:64, :] + mine_far[:64, :]
    out[64:128, :] = theirs[...] + theirs_far[...]
    out[128:, :] = mine[64:, :] + mine_far[64:, :]


def finish_kernel(cotangent, grad_in, own, near, kernel_own, kernel_near, grad_inputs, outputs, grad_kernel, token):
    for at in range(8):
        lanes = slice(at * SIDE, (at + 1) * SIDE)
        grad_inputs[:, lanes] = cotangent[:, lanes] + grad_in[pl.ds(at, 64, stride=8), :]
    outputs[...] = own[...] + near[...]
    grad_kernel[...] = kernel_own[...] + kernel_near[...]
    token[...] = jnp.zeros_like(token)


def final_kernel(gains, total0, total1, total2, total3, out, taps, skip):
    core = jnp.broadcast_to(gains[3:4, :], (64, SIDE)) > 0.5
    place = jnp.broadcast_to(gains[4:5, :], (64, SIDE)) > 0.5
    whole = total0[...] + total1[...] + total2[...] + total3[...]
    near, far = [
        jnp.where(core, pltpu.roll(one, 64, 1), one) for one in (whole[:64], whole[64:128])
    ]
    out[:, :SIDE] = jnp.where(place, far, near)
    out[:, SIDE:] = jnp.where(place, near, far)
    taps[...] = whole[128:131, :64]
    own = jnp.sum(whole[131:132] * gains[8:12, :], axis=1, keepdims=True)
    line = lax.broadcasted_iota(jnp.int32, (4, SIDE), 0)
    lane = lax.broadcasted_iota(jnp.int32, (4, SIDE), 1)
    skip[...] = jnp.sum(jnp.where(line == lane, own, 0.0), axis=0, keepdims=True)[:, :4]


def call(kernel, outs, *args, scalars=0, far=(), far_outs=(), scratch=(), after=(), aliases=()):
    shapes = [shape if not isinstance(shape, tuple) else jax.ShapeDtypeStruct(shape, F32) for shape in outs]
    count = len(args)

    def body(*refs):
        kernel(*refs[:count], *refs[count + len(after) :])

    ins = [SMEM if at < scalars else HBM if at in far else VMEM for at in range(count)]
    places = [HBM if at in far_outs else VMEM for at in range(len(outs))]
    return pl.pallas_call(
        body,
        out_shape=shapes if len(shapes) > 1 else shapes[0],
        in_specs=ins + [pl.BlockSpec(memory_space=pl.ANY)] * len(after),
        out_specs=places if len(shapes) > 1 else places[0],
        scratch_shapes=[shape if not isinstance(shape, tuple) else pltpu.VMEM(shape, F32) for shape in scratch],
        compiler_params=pltpu.CompilerParams(vmem_limit_bytes=20 * 1024 * 1024),
        input_output_aliases=dict(aliases),
        name=kernel.__name__,
    )(*args, *after)


def swapped(value, axes, flip):
    count = lax.axis_size(axes)
    return lax.ppermute(value, axes, [(at, at ^ flip) for at in range(count)])


def turned(value):
    return lax.all_to_all(value, "seq", 0, 0, tiled=True)


def shards(inputs, cotangent, conv_weight, kernel, skip_gain, mix_weight):
    signal = inputs[0]
    grad_out = cotangent[0]
    seq, chan = lax.axis_index("seq"), lax.axis_index("chan")
    place_at = jnp.stack([seq, chan]).astype(jnp.int32)
    into_rows, into_lanes, back_rows, back_lanes, twist = (jnp.asarray(table) for table in tables())
    mix = mix_weight.T

    cot_far = swapped(grad_out, "chan", 2)
    far = jnp.bitwise_xor(lax.shift_right_logical(chan, 1), 1)
    mix_far = swapped(lax.dynamic_slice(mix, (0, 128 * far), (64, 128)), "chan", 2)
    signal_blocks = call(
        blocks_kernel, [(512, SIDE)], signal
    )
    signal_in = turned(signal_blocks.reshape(16, 32, SIDE))
    kernel_spec, gains = call(
        spectrum_kernel, [(512, 256), (16, SIDE)],
        place_at, conv_weight, skip_gain, kernel, into_rows, into_lanes, twist,
        scalars=3, scratch=[(512, SIDE)], after=[signal_blocks],
    )
    weights_into, weights_back = call(
        weights_kernel, [jax.ShapeDtypeStruct((SIDE, 3 * SIDE), BF16)] * 2, place_at, mix, mix_far,
        back_rows, back_lanes, scalars=1, after=[kernel_spec],
    )
    grad_own, grad_other = call(
        grad_act_kernel, [(512, SIDE)] * 2, grad_out, cot_far, weights_into, after=[signal_in]
    )
    grad_near = swapped(grad_other, "chan", 1)
    spec, long_conv, slopes, act = call(
        forward_kernel,
        [(512, 256), (4, SIDE, SIDE), (4, SIDE, SIDE), (16, 64, SIDE)],
        gains, signal_in, kernel_spec, into_rows, into_lanes, back_rows, back_lanes, twist,
        far_outs=(3,), after=[grad_own], scratch=[(16, 32, SIDE), pltpu.SemaphoreType.DMA],
    )
    act = call(
        join_kernel, [(16, 64, SIDE)], act, grad_own, grad_near,
        far=(0,), far_outs=(0,), aliases={0: 0}, scratch=[(16, 32, SIDE), pltpu.SemaphoreType.DMA],
    )
    act_in = turned(act)
    act_own = act_in[:, :32].reshape(512, SIDE)
    act_near = swapped(act_own, "chan", 1)
    grads, small = call(
        slope_kernel, [(4, SIDE, SIDE), (8, SIDE)], gains, act_in, signal_in, long_conv, slopes
    )
    mine, theirs, out_own, out_far = call(
        tail_kernel,
        [(72, SIDE), (64, SIDE), (64, 1024), (64, 1024)],
        act_own, act_near, grad_out, cot_far, signal, weights_back, small,
    )
    grad_long, kernel_local = call(
        backward_kernel,
        [(16, 32, SIDE), (4, LENGTH)],
        grads, spec, kernel_spec, into_rows, into_lanes, back_rows, back_lanes, twist,
        far_outs=(0,), after=[mine], scratch=[(16, 32, SIDE), (512, SIDE), pltpu.SemaphoreType.DMA],
    )
    both = ("dp", "chan")
    total = call(
        merge_kernel, [(136, SIDE)], mine, swapped(mine, both, 4), swapped(theirs, both, 2), swapped(theirs, both, 6),
        after=[kernel_local],
    )
    grad_in = turned(grad_long).reshape(512, SIDE)
    grad_inputs, outputs, grad_kernel, token = call(
        finish_kernel, [(64, 1024), (64, 1024), (4, LENGTH), (8, SIDE)],
        grad_out, grad_in, out_own, swapped(out_far, "chan", 2), kernel_local, swapped(kernel_local, "dp", 1),
    )
    total = total + swapped(total, "seq", 4) + swapped(total, "seq", 12) + swapped(total, "seq", 8)
    grad_mix, grad_conv, grad_skip = call(
        final_kernel, [(64, 256), (3, 64), (1, 4)], gains, total, *(swapped(total, "seq", at) for at in (1, 3, 2)),
        after=[token],
    )
    return (outputs[None], grad_inputs[None], grad_kernel, grad_skip[0], grad_mix.T, grad_conv)


def solution(mesh):
    placed = (
        P("dp", "chan", "seq"),
        P("dp", "chan", "seq"),
        P(None, "chan"),
        P(("chan", "seq"), None),
        P(("chan", "seq")),
        P(None, "chan"),
    )
    return jax.shard_map(
        shards,
        mesh=mesh,
        in_specs=placed,
        out_specs=(
            P("dp", "chan", "seq"),
            P("dp", "chan", "seq"),
            P(("chan", "seq"), None),
            P(("chan", "seq")),
            P(None, "chan"),
            P(None, "chan"),
        ),
        check_vma=False,
    )
```

```python
import functools
import math

import jax
import jax.numpy as jnp
import ml_dtypes
import numpy as np
from jax import lax
from jax.experimental import pallas as pl
from jax.experimental.pallas import tpu as pltpu
from jax.sharding import PartitionSpec as P

SIDE = 128
LENGTH = SIDE * SIDE
F32 = jnp.float32
BF16 = jnp.bfloat16
GELU_SCALE = math.sqrt(2.0 / math.pi)
GELU_CUBE = 0.044715
VMEM = pl.BlockSpec(memory_space=pltpu.VMEM)
SMEM = pl.BlockSpec(memory_space=pltpu.SMEM)
HBM = pl.BlockSpec(memory_space=pltpu.HBM)


def two_parts(table):
    high = table.astype(ml_dtypes.bfloat16)
    low = (table - high.astype(np.float64)).astype(ml_dtypes.bfloat16)
    return high, low


@functools.cache
def tables():
    one = np.arange(SIDE, dtype=np.float64)
    turn = 2.0 * np.pi * np.outer(one + 0.25, one) / SIDE
    rows = np.concatenate([np.cos(turn), -np.sin(turn)], axis=0)
    high, low = two_parts(rows)
    into_rows = np.concatenate([high, low, high], axis=1)
    high, low = two_parts(rows.T / LENGTH)
    back_rows = np.concatenate([high, low, high], axis=1)
    turn = 2.0 * np.pi * np.outer(one, one) / SIDE
    real, imag = np.cos(turn), -np.sin(turn)
    lanes = np.block([[real, imag], [-imag, real]])
    high, low = two_parts(lanes)
    into_lanes = np.concatenate([high, low, high], axis=0)
    high, low = two_parts(lanes.T)
    back_lanes = np.concatenate([high, low, high], axis=0)
    turn = 2.0 * np.pi * np.outer(one + 0.25, one) / LENGTH
    twist = np.stack([np.cos(turn), -np.sin(turn)]).astype(np.float32)
    return into_rows, into_lanes, back_rows, back_lanes, twist


def parts(value):
    high = value.astype(BF16)
    low = (value - high.astype(F32)).astype(BF16)
    return high, low


def dot(left, right, dims=((1,), (0,))):
    return lax.dot_general(left, right, (dims, ((), ())), preferred_element_type=F32)


def forward(pair, into_rows, into_lanes, twist):
    cos, sin = twist[0], twist[1]
    high, low = parts(jnp.concatenate(pair, axis=1))
    step = dot(into_rows[...], jnp.concatenate([high, high, low], axis=0))
    turned = []
    for at in range(len(pair)):
        real = step[:SIDE, at * SIDE : (at + 1) * SIDE]
        imag = step[SIDE:, at * SIDE : (at + 1) * SIDE]
        turned.append(jnp.concatenate([real * cos - imag * sin, real * sin + imag * cos], axis=1))
    high, low = parts(jnp.concatenate(turned, axis=0))
    return dot(jnp.concatenate([high, high, low], axis=1), into_lanes[...])


def backward(spectrum, back_rows, back_lanes, twist):
    cos, sin = twist[0], twist[1]
    count = spectrum.shape[0] // SIDE
    high, low = parts(spectrum)
    step = dot(jnp.concatenate([high, high, low], axis=1), back_lanes[...])
    turned = []
    for at in range(count):
        real = step[at * SIDE : (at + 1) * SIDE, :SIDE]
        imag = step[at * SIDE : (at + 1) * SIDE, SIDE:]
        turned.append(jnp.concatenate([real * cos + imag * sin, imag * cos - real * sin], axis=0))
    high, low = parts(jnp.concatenate(turned, axis=1))
    result = dot(back_rows[...], jnp.concatenate([high, high, low], axis=0))
    return [result[:, at * SIDE : (at + 1) * SIDE] for at in range(count)]


def times(left, right):
    lr, li, rr, ri = left[:, :SIDE], left[:, SIDE:], right[:, :SIDE], right[:, SIDE:]
    return jnp.concatenate([lr * rr - li * ri, lr * ri + li * rr], axis=1)


def times_conj(left, right):
    lr, li, rr, ri = left[:, :SIDE], left[:, SIDE:], right[:, :SIDE], right[:, SIDE:]
    return jnp.concatenate([lr * rr + li * ri, li * rr - lr * ri], axis=1)


def delayed(value, steps):
    row = lax.broadcasted_iota(jnp.int32, value.shape, 0)
    lane = lax.broadcasted_iota(jnp.int32, value.shape, 1)
    turned = pltpu.roll(value, steps, 1)
    above = jnp.where(row == 0, 0.0, pltpu.roll(turned, 1, 0))
    return jnp.where(lane < steps, above, turned)


def advanced(value, steps):
    row = lax.broadcasted_iota(jnp.int32, value.shape, 0)
    lane = lax.broadcasted_iota(jnp.int32, value.shape, 1)
    turned = pltpu.roll(value, SIDE - steps, 1)
    below = jnp.where(row == SIDE - 1, 0.0, pltpu.roll(turned, SIDE - 1, 0))
    return jnp.where(lane >= SIDE - steps, below, turned)


def blocks_kernel(signal, out):
    for at in range(8):
        out[pl.ds(at, 64, stride=8), :] = signal[:, at * SIDE : (at + 1) * SIDE]


def from_blocks(ref):
    return jnp.concatenate([ref[pl.ds(at, 64, stride=8), :] for at in range(8)], axis=1)


def spectrum_kernel(place_at, taps, skip, kernel, into_rows, into_lanes, twist, out, gains, rows):
    for at in range(SIDE):
        rows[pl.ds(at, 4, stride=SIDE), :] = kernel[:, at * SIDE : (at + 1) * SIDE]
    line = lax.broadcasted_iota(jnp.int32, (SIDE, SIDE), 0)
    lane = lax.broadcasted_iota(jnp.int32, (SIDE, SIDE), 1)
    start = (line == 0) & (lane == 0)
    every = [
        rows[at * SIDE : (at + 1) * SIDE, :] + jnp.where(start, skip[at], 0.0) for at in range(4)
    ]
    out[...] = forward(every, into_rows, into_lanes, twist)
    line, lane = line[:16], lane[:16]
    first, chan = 4 * place_at[0], place_at[1]
    result = jnp.where(line == 3, jnp.bitwise_and(chan, 1).astype(F32), 0.0)
    result = jnp.where(line == 4, lax.shift_right_logical(chan, 1).astype(F32), result)
    for row, bit in ((5, 2), (6, 3), (7, 0), (12, 1)):
        flag = jnp.bitwise_and(lax.shift_right_logical(place_at[0], bit), 1)
        result = jnp.where(line == row, flag.astype(F32), result)
    result = jnp.where((line >= 8) & (line < 12) & (lane == first + line - 8), 1.0, result)
    for tap in range(3):
        for at in range(4):
            result = jnp.where((line == tap) & (lane == at), taps[tap, first + at], result)
    gains[...] = result


def weights_kernel(place_at, mix, mix_far, _rows, _lanes, into, back):
    chan = place_at[1]
    start = pl.multiple_of(128 * lax.shift_right_logical(chan, 1), 128)
    both = jnp.concatenate([mix[:, pl.ds(start, 128)], mix_far[...]], axis=0)
    both = pltpu.roll(both, 64 * jnp.bitwise_and(chan, 1), 1)
    high, low = parts(both)
    back[...] = jnp.concatenate([high, low, high], axis=1)
    high, low = parts(both.T)
    into[...] = jnp.concatenate([high, low, high], axis=1)


def grad_act_kernel(cot, cot_far, weights, own, other):
    for half in range(4):
        lanes = slice(half * 256, (half + 1) * 256)
        high, low = parts(jnp.concatenate([cot[:, lanes], cot_far[:, lanes]], axis=0))
        result = dot(weights[...], jnp.concatenate([high, high, low], axis=0))
        for at in range(2):
            place = pl.ds(2 * half + at, 64, stride=8)
            own[place, :] = result[:64, at * SIDE : (at + 1) * SIDE]
            other[place, :] = result[64:, at * SIDE : (at + 1) * SIDE]


def channel(ref, at):
    return ref[:, at * 8 : (at + 1) * 8, :].reshape(SIDE, SIDE)


def gains_of(gains, at):
    return [jnp.broadcast_to(gains[tap : tap + 1, at : at + 1], (SIDE, SIDE)) for tap in range(3)]


def moved(copies):
    for one in copies:
        one.start()
    return copies


def forward_kernel(
    gains, signal, kernel_spec, into_rows, into_lanes, back_rows, back_lanes, twist,
    spec, long_conv, slopes, act_out, act, sem,
):
    spectrum = forward([channel(signal, at) for at in range(4)], into_rows, into_lanes, twist)
    spec[...] = spectrum
    result = backward(times(spectrum, kernel_spec[...]), back_rows, back_lanes, twist)
    for index in range(4):
        taps = gains_of(gains, index)
        whole = result[index]
        long_conv[index] = whole
        value = taps[2] * whole + taps[1] * delayed(whole, 1) + taps[0] * delayed(whole, 2)
        square = value * value
        half = 0.5 + 0.5 * jnp.tanh(value * (GELU_SCALE + GELU_SCALE * GELU_CUBE * square))
        act[:, index * 8 : (index + 1) * 8, :] = (value * half).reshape(16, 8, SIDE)
        slopes[index] = half + half * (1.0 - half) * value * (
            2.0 * GELU_SCALE + 6.0 * GELU_SCALE * GELU_CUBE * square
        )
    copy = pltpu.make_async_copy(act, act_out.at[:, pl.ds(0, 32), :], sem)
    copy.start()
    copy.wait()


def join_kernel(act, own, near, out, total, sem):
    total[...] = (own[...] + near[...]).reshape(16, 32, SIDE)
    copy = pltpu.make_async_copy(total, out.at[:, pl.ds(32, 32), :], sem)
    copy.start()
    copy.wait()


def slope_kernel(gains, grad_act, signal, long_conv, slopes, grads, small):
    small[...] = jnp.zeros_like(small)
    for index in range(4):
        taps = gains_of(gains, index)
        grad = channel(grad_act, 4 + index) * slopes[index]
        later = [advanced(grad, 2), advanced(grad, 1), grad]
        grads[index] = taps[0] * later[0] + taps[1] * later[1] + taps[2] * later[2]
        pairs = [one * long_conv[index] for one in later] + [grads[index] * channel(signal, index)]
        sums = jnp.concatenate([jnp.sum(one, axis=0, keepdims=True) for one in pairs], axis=0)
        small[:4, :] = small[:4, :] + jnp.sum(sums, axis=1, keepdims=True) * gains[8 + index : 9 + index, :]


def backward_kernel(
    grads, spec, kernel_spec, into_rows, into_lanes, back_rows, back_lanes, twist,
    grad_in, kernel_out, rows,
):
    spectrum = forward([grads[at] for at in range(4)], into_rows, into_lanes, twist)
    result = backward(times_conj(spectrum, kernel_spec[...]), back_rows, back_lanes, twist)
    for at in range(4):
        grad_in[:, at * 8 : (at + 1) * 8, :] = result[at].reshape(16, 8, SIDE)
    result = backward(times_conj(spectrum, spec[...]), back_rows, back_lanes, twist)
    for at in range(4):
        rows[at * SIDE : (at + 1) * SIDE, :] = result[at]
    for at in range(SIDE):
        kernel_out[:, at * SIDE : (at + 1) * SIDE] = rows[pl.ds(at, 4, stride=SIDE), :]


def tail_kernel(act, act_near, cot, cot_far, signal, weights, small, mine, theirs, out, out_far):
    active = jnp.concatenate([from_blocks(act), from_blocks(act_near)], axis=0)
    act_high, act_low = parts(active)
    high, low = parts(jnp.concatenate([cot[...], cot_far[...]], axis=0))
    result = dot(
        jnp.concatenate([high, low, high], axis=1),
        jnp.concatenate([act_high, act_high, act_low], axis=1),
        ((1,), (1,)),
    )
    mine[:64, :] = result[:64]
    mine[64:, :] = small[...]
    theirs[...] = result[64:]
    mixed = dot(weights[...], jnp.concatenate([act_high, act_high, act_low], axis=0))
    out[...] = signal[...] + mixed[:64]
    out_far[...] = mixed[64:]


def flag(gains, row, shape):
    return jnp.broadcast_to(gains[row : row + 1, :], shape) > 0.5


def relative(blocks, low, high):
    blocks = [jnp.where(low, blocks[at ^ 1], blocks[at]) for at in range(4)]
    return [jnp.where(high, blocks[at ^ 2], blocks[at]) for at in range(4)]


def merge_kernel(gains, grad, mine, mine_far, theirs_far, theirs, out0, out1, out2, out3):
    total = [
        mine[:64, :] + mine_far[:64, :],
        theirs[...] + theirs_far[...],
        mine[64:, :] + mine_far[64:, :],
    ]
    shape = (SIDE, SIDE)
    blocks = [grad[at * 4 : (at + 1) * 4].reshape(SIDE, SIDE) for at in range(4)]
    blocks = relative(blocks, flag(gains, 5, shape), flag(gains, 6, shape))
    for out, block in zip((out0, out1, out2, out3), blocks):
        out[:64, :] = total[0]
        out[64:128, :] = total[1]
        out[128:136, :] = total[2]
        out[136:, :] = block


def sum_kernel(gains, in0, in2, in3, in1, out0, out1, out2, out3):
    whole = in0[:136, :] + in1[:136, :] + in2[:136, :] + in3[:136, :]
    outs = (out0, out1, out2, out3)
    for out in outs:
        out[:136, :] = whole
    shape = (32, SIDE)
    low, high = flag(gains, 7, shape), flag(gains, 12, shape)
    for near, ref in enumerate((in0, in1, in2, in3)):
        blocks = relative([ref[136 + 32 * at : 168 + 32 * at, :] for at in range(4)], low, high)
        for out, block in zip(outs, blocks):
            out[136 + 32 * near : 168 + 32 * near, :] = block


def finish_kernel(own, near, kernel_own, kernel_near, outputs, grad_kernel, token):
    outputs[...] = own[...] + near[...]
    grad_kernel[...] = kernel_own[...] + kernel_near[...]
    token[...] = jnp.zeros_like(token)


def final_kernel(gains, cotangent, in0, in2, in3, in1, out, taps, skip, grad_inputs, rows):
    core, place = flag(gains, 3, (64, SIDE)), flag(gains, 4, (64, SIDE))
    whole = in0[:136, :] + in1[:136, :] + in2[:136, :] + in3[:136, :]
    near, far = [
        jnp.where(core, pltpu.roll(one, 64, 1), one) for one in (whole[:64], whole[64:128])
    ]
    out[:, :SIDE] = jnp.where(place, far, near)
    out[:, SIDE:] = jnp.where(place, near, far)
    taps[...] = whole[128:131, :64]
    own = jnp.sum(whole[131:132] * gains[8:12, :], axis=1, keepdims=True)
    line = lax.broadcasted_iota(jnp.int32, (4, SIDE), 0)
    lane = lax.broadcasted_iota(jnp.int32, (4, SIDE), 1)
    skip[...] = jnp.sum(jnp.where(line == lane, own, 0.0), axis=0, keepdims=True)[:, :4]
    shape = (SIDE, SIDE)
    by_x = relative([ref[136:, :] for ref in (in0, in1, in2, in3)], flag(gains, 7, shape), flag(gains, 12, shape))
    shape = (32, SIDE)
    low, high = flag(gains, 5, shape), flag(gains, 6, shape)
    for x, column in enumerate(by_x):
        column = relative([column[32 * at : 32 * at + 32] for at in range(4)], low, high)
        for z in range(4):
            rows[(4 * z + x) * 32 : (4 * z + x + 1) * 32, :] = column[z]
    for at in range(8):
        lanes = slice(at * SIDE, (at + 1) * SIDE)
        grad_inputs[:, lanes] = cotangent[:, lanes] + rows[pl.ds(at, 64, stride=8), :]


def call(kernel, outs, *args, scalars=0, far=(), far_outs=(), scratch=(), after=(), aliases=()):
    shapes = [shape if not isinstance(shape, tuple) else jax.ShapeDtypeStruct(shape, F32) for shape in outs]
    count = len(args)

    def body(*refs):
        kernel(*refs[:count], *refs[count + len(after) :])

    ins = [SMEM if at < scalars else HBM if at in far else VMEM for at in range(count)]
    places = [HBM if at in far_outs else VMEM for at in range(len(outs))]
    return pl.pallas_call(
        body,
        out_shape=shapes if len(shapes) > 1 else shapes[0],
        in_specs=ins + [pl.BlockSpec(memory_space=pl.ANY)] * len(after),
        out_specs=places if len(shapes) > 1 else places[0],
        scratch_shapes=[shape if not isinstance(shape, tuple) else pltpu.VMEM(shape, F32) for shape in scratch],
        compiler_params=pltpu.CompilerParams(vmem_limit_bytes=20 * 1024 * 1024),
        input_output_aliases=dict(aliases),
        name=kernel.__name__,
    )(*args, *after)


def swapped(value, axes, flip):
    count = lax.axis_size(axes)
    return lax.ppermute(value, axes, [(at, at ^ flip) for at in range(count)])


def turned(value):
    return lax.all_to_all(value, "seq", 0, 0, tiled=True)


def shards(inputs, cotangent, conv_weight, kernel, skip_gain, mix_weight):
    signal = inputs[0]
    grad_out = cotangent[0]
    seq, chan = lax.axis_index("seq"), lax.axis_index("chan")
    place_at = jnp.stack([seq, chan]).astype(jnp.int32)
    into_rows, into_lanes, back_rows, back_lanes, twist = (jnp.asarray(table) for table in tables())
    mix = mix_weight.T

    cot_far = swapped(grad_out, "chan", 2)
    far = jnp.bitwise_xor(lax.shift_right_logical(chan, 1), 1)
    mix_far = swapped(lax.dynamic_slice(mix, (0, 128 * far), (64, 128)), "chan", 2)
    signal_blocks = call(
        blocks_kernel, [(512, SIDE)], signal
    )
    signal_in = turned(signal_blocks.reshape(16, 32, SIDE))
    kernel_spec, gains = call(
        spectrum_kernel, [(512, 256), (16, SIDE)],
        place_at, conv_weight, skip_gain, kernel, into_rows, into_lanes, twist,
        scalars=3, scratch=[(512, SIDE)], after=[signal_blocks],
    )
    weights_into, weights_back = call(
        weights_kernel, [jax.ShapeDtypeStruct((SIDE, 3 * SIDE), BF16)] * 2, place_at, mix, mix_far,
        back_rows, back_lanes, scalars=1, after=[kernel_spec],
    )
    grad_own, grad_other = call(
        grad_act_kernel, [(512, SIDE)] * 2, grad_out, cot_far, weights_into, after=[signal_in]
    )
    grad_near = swapped(grad_other, "chan", 1)
    spec, long_conv, slopes, act = call(
        forward_kernel,
        [(512, 256), (4, SIDE, SIDE), (4, SIDE, SIDE), (16, 64, SIDE)],
        gains, signal_in, kernel_spec, into_rows, into_lanes, back_rows, back_lanes, twist,
        far_outs=(3,), after=[grad_own], scratch=[(16, 32, SIDE), pltpu.SemaphoreType.DMA],
    )
    act = call(
        join_kernel, [(16, 64, SIDE)], act, grad_own, grad_near,
        far=(0,), far_outs=(0,), aliases={0: 0}, scratch=[(16, 32, SIDE), pltpu.SemaphoreType.DMA],
    )
    act_in = turned(act)
    act_own = act_in[:, :32].reshape(512, SIDE)
    act_near = swapped(act_own, "chan", 1)
    grads, small = call(
        slope_kernel, [(4, SIDE, SIDE), (8, SIDE)], gains, act_in, signal_in, long_conv, slopes
    )
    mine, theirs, out_own, out_far = call(
        tail_kernel,
        [(72, SIDE), (64, SIDE), (64, 1024), (64, 1024)],
        act_own, act_near, grad_out, cot_far, signal, weights_back, small,
    )
    grad_long, kernel_local = call(
        backward_kernel,
        [(16, 32, SIDE), (4, LENGTH)],
        grads, spec, kernel_spec, into_rows, into_lanes, back_rows, back_lanes, twist,
        after=[mine], scratch=[(512, SIDE)],
    )
    both = ("dp", "chan")
    far_theirs = [swapped(theirs, both, flip) for flip in (6, 2)]
    sends = call(
        merge_kernel, [(264, SIDE)] * 4, gains, grad_long, mine, swapped(mine, both, 4), *far_theirs
    )
    sends = call(
        sum_kernel, [(264, SIDE)] * 4,
        gains, sends[0], *(swapped(sends[at], "seq", 4 * at) for at in (2, 3, 1)),
    )
    outputs, grad_kernel, token = call(
        finish_kernel, [(64, 1024), (4, LENGTH), (8, SIDE)],
        out_own, swapped(out_far, "chan", 2), kernel_local, swapped(kernel_local, "dp", 1),
    )
    grad_mix, grad_conv, grad_skip, grad_inputs = call(
        final_kernel, [(64, 256), (3, 64), (1, 4), (64, 1024)],
        gains, grad_out, sends[0], *(swapped(sends[at], "seq", at) for at in (2, 3, 1)),
        scratch=[(512, SIDE)], after=[token],
    )
    return (outputs[None], grad_inputs[None], grad_kernel, grad_skip[0], grad_mix.T, grad_conv)


def solution(mesh):
    placed = (
        P("dp", "chan", "seq"),
        P("dp", "chan", "seq"),
        P(None, "chan"),
        P(("chan", "seq"), None),
        P(("chan", "seq")),
        P(None, "chan"),
    )
    return jax.shard_map(
        shards,
        mesh=mesh,
        in_specs=placed,
        out_specs=(
            P("dp", "chan", "seq"),
            P("dp", "chan", "seq"),
            P(("chan", "seq"), None),
            P(("chan", "seq")),
            P(None, "chan"),
            P(None, "chan"),
        ),
        check_vma=False,
    )
```

```python
import functools
import math

import jax
import jax.numpy as jnp
import ml_dtypes
import numpy as np
from jax import lax
from jax.experimental import pallas as pl
from jax.experimental.pallas import tpu as pltpu
from jax.sharding import PartitionSpec as P

SIDE = 128
LENGTH = SIDE * SIDE
F32 = jnp.float32
BF16 = jnp.bfloat16
GELU_SCALE = math.sqrt(2.0 / math.pi)
GELU_CUBE = 0.044715
VMEM = pl.BlockSpec(memory_space=pltpu.VMEM)
SMEM = pl.BlockSpec(memory_space=pltpu.SMEM)
HBM = pl.BlockSpec(memory_space=pltpu.HBM)


def two_parts(table):
    high = table.astype(ml_dtypes.bfloat16)
    low = (table - high.astype(np.float64)).astype(ml_dtypes.bfloat16)
    return high, low


@functools.cache
def tables():
    one = np.arange(SIDE, dtype=np.float64)
    turn = 2.0 * np.pi * np.outer(one + 0.25, one) / SIDE
    rows = np.concatenate([np.cos(turn), -np.sin(turn)], axis=0)
    high, low = two_parts(rows)
    into_rows = np.concatenate([high, low, high], axis=1)
    high, low = two_parts(rows.T / LENGTH)
    back_rows = np.concatenate([high, low, high], axis=1)
    turn = 2.0 * np.pi * np.outer(one, one) / SIDE
    real, imag = np.cos(turn), -np.sin(turn)
    lanes = np.block([[real, imag], [-imag, real]])
    high, low = two_parts(lanes)
    into_lanes = np.concatenate([high, low, high], axis=0)
    high, low = two_parts(lanes.T)
    back_lanes = np.concatenate([high, low, high], axis=0)
    turn = 2.0 * np.pi * np.outer(one + 0.25, one) / LENGTH
    twist = np.stack([np.cos(turn), -np.sin(turn)]).astype(np.float32)
    return into_rows, into_lanes, back_rows, back_lanes, twist


def parts(value):
    high = value.astype(BF16)
    low = (value - high.astype(F32)).astype(BF16)
    return high, low


def dot(left, right, dims=((1,), (0,))):
    return lax.dot_general(left, right, (dims, ((), ())), preferred_element_type=F32)


def forward(pair, into_rows, into_lanes, twist):
    cos, sin = twist[0], twist[1]
    high, low = parts(jnp.concatenate(pair, axis=1))
    step = dot(into_rows[...], jnp.concatenate([high, high, low], axis=0))
    turned = []
    for at in range(len(pair)):
        real = step[:SIDE, at * SIDE : (at + 1) * SIDE]
        imag = step[SIDE:, at * SIDE : (at + 1) * SIDE]
        turned.append(jnp.concatenate([real * cos - imag * sin, real * sin + imag * cos], axis=1))
    high, low = parts(jnp.concatenate(turned, axis=0))
    return dot(jnp.concatenate([high, high, low], axis=1), into_lanes[...])


def backward(spectrum, back_rows, back_lanes, twist):
    cos, sin = twist[0], twist[1]
    count = spectrum.shape[0] // SIDE
    high, low = parts(spectrum)
    step = dot(jnp.concatenate([high, high, low], axis=1), back_lanes[...])
    turned = []
    for at in range(count):
        real = step[at * SIDE : (at + 1) * SIDE, :SIDE]
        imag = step[at * SIDE : (at + 1) * SIDE, SIDE:]
        turned.append(jnp.concatenate([real * cos + imag * sin, imag * cos - real * sin], axis=0))
    high, low = parts(jnp.concatenate(turned, axis=1))
    result = dot(back_rows[...], jnp.concatenate([high, high, low], axis=0))
    return [result[:, at * SIDE : (at + 1) * SIDE] for at in range(count)]


def times(left, right):
    lr, li, rr, ri = left[:, :SIDE], left[:, SIDE:], right[:, :SIDE], right[:, SIDE:]
    return jnp.concatenate([lr * rr - li * ri, lr * ri + li * rr], axis=1)


def times_conj(left, right):
    lr, li, rr, ri = left[:, :SIDE], left[:, SIDE:], right[:, :SIDE], right[:, SIDE:]
    return jnp.concatenate([lr * rr + li * ri, li * rr - lr * ri], axis=1)


def delayed(value, steps):
    row = lax.broadcasted_iota(jnp.int32, value.shape, 0)
    lane = lax.broadcasted_iota(jnp.int32, value.shape, 1)
    turned = pltpu.roll(value, steps, 1)
    above = jnp.where(row == 0, 0.0, pltpu.roll(turned, 1, 0))
    return jnp.where(lane < steps, above, turned)


def advanced(value, steps):
    row = lax.broadcasted_iota(jnp.int32, value.shape, 0)
    lane = lax.broadcasted_iota(jnp.int32, value.shape, 1)
    turned = pltpu.roll(value, SIDE - steps, 1)
    below = jnp.where(row == SIDE - 1, 0.0, pltpu.roll(turned, SIDE - 1, 0))
    return jnp.where(lane >= SIDE - steps, below, turned)


def blocks_kernel(signal, out):
    for at in range(8):
        out[pl.ds(at, 64, stride=8), :] = signal[:, at * SIDE : (at + 1) * SIDE]


def from_blocks(ref):
    return jnp.concatenate([ref[pl.ds(at, 64, stride=8), :] for at in range(8)], axis=1)


def spectrum_kernel(place_at, taps, skip, kernel, into_rows, into_lanes, twist, out, gains, rows):
    for at in range(SIDE):
        rows[pl.ds(at, 4, stride=SIDE), :] = kernel[:, at * SIDE : (at + 1) * SIDE]
    line = lax.broadcasted_iota(jnp.int32, (SIDE, SIDE), 0)
    lane = lax.broadcasted_iota(jnp.int32, (SIDE, SIDE), 1)
    start = (line == 0) & (lane == 0)
    every = [
        rows[at * SIDE : (at + 1) * SIDE, :] + jnp.where(start, skip[at], 0.0) for at in range(4)
    ]
    out[...] = forward(every, into_rows, into_lanes, twist)
    line, lane = line[:16], lane[:16]
    first, chan = 4 * place_at[0], place_at[1]
    result = jnp.where(line == 3, jnp.bitwise_and(chan, 1).astype(F32), 0.0)
    result = jnp.where(line == 4, lax.shift_right_logical(chan, 1).astype(F32), result)
    turn = 2 * jnp.bitwise_and(chan, 1)
    for row, bit in ((5, 2), (6, 3), (7, 0), (12, 1)):
        bit = bit + turn if bit < 2 else bit - turn
        one = jnp.bitwise_and(lax.shift_right_logical(place_at[0], bit), 1)
        result = jnp.where(line == row, one.astype(F32), result)
    result = jnp.where((line >= 8) & (line < 12) & (lane == first + line - 8), 1.0, result)
    for tap in range(3):
        for at in range(4):
            result = jnp.where((line == tap) & (lane == at), taps[tap, first + at], result)
    gains[...] = result


def weights_kernel(place_at, mix, mix_far, _rows, _lanes, into, back):
    chan = place_at[1]
    start = pl.multiple_of(128 * lax.shift_right_logical(chan, 1), 128)
    both = jnp.concatenate([mix[:, pl.ds(start, 128)], mix_far[...]], axis=0)
    both = pltpu.roll(both, 64 * jnp.bitwise_and(chan, 1), 1)
    high, low = parts(both)
    back[...] = jnp.concatenate([high, low, high], axis=1)
    high, low = parts(both.T)
    into[...] = jnp.concatenate([high, low, high], axis=1)


def grad_act_kernel(cot, cot_far, weights, own, other):
    for half in range(4):
        lanes = slice(half * 256, (half + 1) * 256)
        high, low = parts(jnp.concatenate([cot[:, lanes], cot_far[:, lanes]], axis=0))
        result = dot(weights[...], jnp.concatenate([high, high, low], axis=0))
        for at in range(2):
            place = pl.ds(2 * half + at, 64, stride=8)
            own[place, :] = result[:64, at * SIDE : (at + 1) * SIDE]
            other[place, :] = result[64:, at * SIDE : (at + 1) * SIDE]


def channel(ref, at):
    return ref[:, at * 8 : (at + 1) * 8, :].reshape(SIDE, SIDE)


def gains_of(gains, at):
    return [jnp.broadcast_to(gains[tap : tap + 1, at : at + 1], (SIDE, SIDE)) for tap in range(3)]


def moved(copies):
    for one in copies:
        one.start()
    return copies


def forward_kernel(
    gains, signal, kernel_spec, into_rows, into_lanes, back_rows, back_lanes, twist,
    spec, long_conv, slopes, act_out, act, sem,
):
    spectrum = forward([channel(signal, at) for at in range(4)], into_rows, into_lanes, twist)
    spec[...] = spectrum
    result = backward(times(spectrum, kernel_spec[...]), back_rows, back_lanes, twist)
    for index in range(4):
        taps = gains_of(gains, index)
        whole = result[index]
        long_conv[index] = whole
        value = taps[2] * whole + taps[1] * delayed(whole, 1) + taps[0] * delayed(whole, 2)
        square = value * value
        half = 0.5 + 0.5 * jnp.tanh(value * (GELU_SCALE + GELU_SCALE * GELU_CUBE * square))
        act[:, index * 8 : (index + 1) * 8, :] = (value * half).reshape(16, 8, SIDE)
        slopes[index] = half + half * (1.0 - half) * value * (
            2.0 * GELU_SCALE + 6.0 * GELU_SCALE * GELU_CUBE * square
        )
    copy = pltpu.make_async_copy(act, act_out.at[:, pl.ds(0, 32), :], sem)
    copy.start()
    copy.wait()


def join_kernel(act, own, near, out, total, sem):
    total[...] = (own[...] + near[...]).reshape(16, 32, SIDE)
    copy = pltpu.make_async_copy(total, out.at[:, pl.ds(32, 32), :], sem)
    copy.start()
    copy.wait()


def slope_kernel(gains, grad_act, signal, long_conv, slopes, grads, small):
    small[...] = jnp.zeros_like(small)
    for index in range(4):
        taps = gains_of(gains, index)
        grad = channel(grad_act, 4 + index) * slopes[index]
        later = [advanced(grad, 2), advanced(grad, 1), grad]
        grads[index] = taps[0] * later[0] + taps[1] * later[1] + taps[2] * later[2]
        pairs = [one * long_conv[index] for one in later] + [grads[index] * channel(signal, index)]
        sums = jnp.concatenate([jnp.sum(one, axis=0, keepdims=True) for one in pairs], axis=0)
        small[:4, :] = small[:4, :] + jnp.sum(sums, axis=1, keepdims=True) * gains[8 + index : 9 + index, :]


def backward_kernel(
    grads, spec, kernel_spec, into_rows, into_lanes, back_rows, back_lanes, twist,
    grad_in, kernel_out, rows,
):
    spectrum = forward([grads[at] for at in range(4)], into_rows, into_lanes, twist)
    result = backward(times_conj(spectrum, kernel_spec[...]), back_rows, back_lanes, twist)
    for at in range(4):
        grad_in[:, at * 8 : (at + 1) * 8, :] = result[at].reshape(16, 8, SIDE)
    result = backward(times_conj(spectrum, spec[...]), back_rows, back_lanes, twist)
    for at in range(4):
        rows[at * SIDE : (at + 1) * SIDE, :] = result[at]
    for at in range(SIDE):
        kernel_out[:, at * SIDE : (at + 1) * SIDE] = rows[pl.ds(at, 4, stride=SIDE), :]


def tail_kernel(act, act_near, cot, cot_far, signal, weights, small, mine, theirs, out, out_far):
    active = jnp.concatenate([from_blocks(act), from_blocks(act_near)], axis=0)
    act_high, act_low = parts(active)
    high, low = parts(jnp.concatenate([cot[...], cot_far[...]], axis=0))
    result = dot(
        jnp.concatenate([high, low, high], axis=1),
        jnp.concatenate([act_high, act_high, act_low], axis=1),
        ((1,), (1,)),
    )
    mine[:64, :] = result[:64]
    mine[64:, :] = small[...]
    theirs[...] = result[64:]
    mixed = dot(weights[...], jnp.concatenate([act_high, act_high, act_low], axis=0))
    out[...] = signal[...] + mixed[:64]
    out_far[...] = mixed[64:]


def flag(gains, row, shape):
    return jnp.broadcast_to(gains[row : row + 1, :], shape) > 0.5


def relative(blocks, low, high):
    blocks = [jnp.where(low, blocks[at ^ 1], blocks[at]) for at in range(4)]
    return [jnp.where(high, blocks[at ^ 2], blocks[at]) for at in range(4)]


def by_core(grid, swap):
    return [[jnp.where(swap, grid[b][a], grid[a][b]) if a != b else grid[a][a] for b in range(4)] for a in range(4)]


def merge_kernel(gains, grad, mine, mine_far, theirs_far, theirs, out0, out1, out2, out3):
    total = [
        mine[:64, :] + mine_far[:64, :],
        theirs[...] + theirs_far[...],
        mine[64:, :] + mine_far[64:, :],
    ]
    shape = (SIDE, SIDE)
    grid = by_core([[grad[4 * a + b] for b in range(4)] for a in range(4)], flag(gains, 3, (32, SIDE)))
    blocks = relative([jnp.concatenate(row, axis=0) for row in grid], flag(gains, 5, shape), flag(gains, 6, shape))
    for out, block in zip((out0, out1, out2, out3), blocks):
        out[:64, :] = total[0]
        out[64:128, :] = total[1]
        out[128:136, :] = total[2]
        out[136:, :] = block


def sum_kernel(gains, in0, in2, in3, in1, out0, out1, out2, out3):
    whole = in0[:136, :] + in1[:136, :] + in2[:136, :] + in3[:136, :]
    outs = (out0, out1, out2, out3)
    for out in outs:
        out[:136, :] = whole
    shape = (32, SIDE)
    low, high = flag(gains, 7, shape), flag(gains, 12, shape)
    for near, ref in enumerate((in0, in1, in2, in3)):
        blocks = relative([ref[136 + 32 * at : 168 + 32 * at, :] for at in range(4)], low, high)
        for out, block in zip(outs, blocks):
            out[136 + 32 * near : 168 + 32 * near, :] = block


def outputs_kernel(own, near, outputs, token):
    outputs[...] = own[...] + near[...]
    token[...] = jnp.zeros_like(token)


def finish_kernel(own, near, grad_kernel):
    grad_kernel[...] = own[...] + near[...]


def final_kernel(gains, cotangent, in0, in2, in3, in1, out, taps, skip, grad_inputs, token, rows):
    core, place = flag(gains, 3, (64, SIDE)), flag(gains, 4, (64, SIDE))
    whole = in0[:136, :] + in1[:136, :] + in2[:136, :] + in3[:136, :]
    near, far = [
        jnp.where(core, pltpu.roll(one, 64, 1), one) for one in (whole[:64], whole[64:128])
    ]
    out[:, :SIDE] = jnp.where(place, far, near)
    out[:, SIDE:] = jnp.where(place, near, far)
    token[...] = jnp.zeros_like(token)
    taps[...] = whole[128:131, :64]
    own = jnp.sum(whole[131:132] * gains[8:12, :], axis=1, keepdims=True)
    line = lax.broadcasted_iota(jnp.int32, (4, SIDE), 0)
    lane = lax.broadcasted_iota(jnp.int32, (4, SIDE), 1)
    skip[...] = jnp.sum(jnp.where(line == lane, own, 0.0), axis=0, keepdims=True)[:, :4]
    shape = (SIDE, SIDE)
    columns = relative([ref[136:, :] for ref in (in0, in1, in2, in3)], flag(gains, 7, shape), flag(gains, 12, shape))
    shape = (32, SIDE)
    low, high = flag(gains, 5, shape), flag(gains, 6, shape)
    columns = [relative([column[32 * at : 32 * at + 32] for at in range(4)], low, high) for column in columns]
    grid = by_core([[columns[b][a] for b in range(4)] for a in range(4)], flag(gains, 3, shape))
    for z in range(4):
        for x in range(4):
            rows[(4 * z + x) * 32 : (4 * z + x + 1) * 32, :] = grid[z][x]
    for at in range(8):
        lanes = slice(at * SIDE, (at + 1) * SIDE)
        grad_inputs[:, lanes] = cotangent[:, lanes] + rows[pl.ds(at, 64, stride=8), :]


def call(kernel, outs, *args, scalars=0, far=(), far_outs=(), scratch=(), after=(), aliases=()):
    shapes = [shape if not isinstance(shape, tuple) else jax.ShapeDtypeStruct(shape, F32) for shape in outs]
    count = len(args)

    def body(*refs):
        kernel(*refs[:count], *refs[count + len(after) :])

    ins = [SMEM if at < scalars else HBM if at in far else VMEM for at in range(count)]
    places = [HBM if at in far_outs else VMEM for at in range(len(outs))]
    return pl.pallas_call(
        body,
        out_shape=shapes if len(shapes) > 1 else shapes[0],
        in_specs=ins + [pl.BlockSpec(memory_space=pl.ANY)] * len(after),
        out_specs=places if len(shapes) > 1 else places[0],
        scratch_shapes=[shape if not isinstance(shape, tuple) else pltpu.VMEM(shape, F32) for shape in scratch],
        compiler_params=pltpu.CompilerParams(vmem_limit_bytes=20 * 1024 * 1024),
        input_output_aliases=dict(aliases),
        name=kernel.__name__,
        cost_estimate=pl.CostEstimate(flops=20000000000, bytes_accessed=0, transcendentals=0) if kernel is forward_kernel else None,
    )(*args, *after)


def swapped(value, axes, flip):
    count = lax.axis_size(axes)
    return lax.ppermute(value, axes, [(at, at ^ flip) for at in range(count)])


def crossed(value, flip, second):
    pairs = []
    for seq in range(16):
        for chan in range(4):
            there = seq ^ (flip if (chan + second) % 2 else 4 * flip)
            pairs.append((4 * seq + chan, 4 * there + chan))
    return lax.ppermute(value, ("seq", "chan"), pairs)


def turned(value):
    return lax.all_to_all(value, "seq", 0, 0, tiled=True)


def shards(inputs, cotangent, conv_weight, kernel, skip_gain, mix_weight):
    signal = inputs[0]
    grad_out = cotangent[0]
    seq, chan = lax.axis_index("seq"), lax.axis_index("chan")
    place_at = jnp.stack([seq, chan]).astype(jnp.int32)
    into_rows, into_lanes, back_rows, back_lanes, twist = (jnp.asarray(table) for table in tables())
    mix = mix_weight.T

    cot_far = swapped(grad_out, "chan", 2)
    far = jnp.bitwise_xor(lax.shift_right_logical(chan, 1), 1)
    mix_far = swapped(lax.dynamic_slice(mix, (0, 128 * far), (64, 128)), "chan", 2)
    signal_blocks = call(
        blocks_kernel, [(512, SIDE)], signal
    )
    signal_in = turned(signal_blocks.reshape(16, 32, SIDE))
    kernel_spec, gains = call(
        spectrum_kernel, [(512, 256), (16, SIDE)],
        place_at, conv_weight, skip_gain, kernel, into_rows, into_lanes, twist,
        scalars=3, scratch=[(512, SIDE)], after=[signal_blocks],
    )
    weights_into, weights_back = call(
        weights_kernel, [jax.ShapeDtypeStruct((SIDE, 3 * SIDE), BF16)] * 2, place_at, mix, mix_far,
        back_rows, back_lanes, scalars=1,
    )
    grad_own, grad_other = call(
        grad_act_kernel, [(512, SIDE)] * 2, grad_out, cot_far, weights_into
    )
    grad_near = swapped(grad_other, "chan", 1)
    spec, long_conv, slopes, act = call(
        forward_kernel,
        [(512, 256), (4, SIDE, SIDE), (4, SIDE, SIDE), (16, 64, SIDE)],
        gains, signal_in, kernel_spec, into_rows, into_lanes, back_rows, back_lanes, twist,
        far_outs=(3,), after=[grad_own], scratch=[(16, 32, SIDE), pltpu.SemaphoreType.DMA],
    )
    act = call(
        join_kernel, [(16, 64, SIDE)], act, grad_own, grad_near,
        far=(0,), far_outs=(0,), aliases={0: 0}, scratch=[(16, 32, SIDE), pltpu.SemaphoreType.DMA],
    )
    act_in = turned(act)
    act_own = act_in[:, :32].reshape(512, SIDE)
    act_near = swapped(act_own, "chan", 1)
    grads, small = call(
        slope_kernel, [(4, SIDE, SIDE), (8, SIDE)], gains, act_in, signal_in, long_conv, slopes
    )
    mine, theirs, out_own, out_far = call(
        tail_kernel,
        [(72, SIDE), (64, SIDE), (64, 1024), (64, 1024)],
        act_own, act_near, grad_out, cot_far, signal, weights_back, small,
    )
    grad_long, kernel_local = call(
        backward_kernel,
        [(16, 32, SIDE), (4, LENGTH)],
        grads, spec, kernel_spec, into_rows, into_lanes, back_rows, back_lanes, twist,
        after=[mine], scratch=[(512, SIDE)],
    )
    both = ("dp", "chan")
    far_theirs = [swapped(theirs, both, flip) for flip in (6, 2)]
    sends = call(
        merge_kernel, [(264, SIDE)] * 4, gains, grad_long, mine, swapped(mine, both, 4), *far_theirs
    )
    sends = call(
        sum_kernel, [(264, SIDE)] * 4,
        gains, sends[0], *(crossed(sends[at], at, 0) for at in (2, 3, 1)),
    )
    outputs, token = call(
        outputs_kernel, [(64, 1024), (8, SIDE)], out_own, swapped(out_far, "chan", 2)
    )
    grad_mix, grad_conv, grad_skip, grad_inputs, token = call(
        final_kernel, [(64, 256), (3, 64), (1, 4), (64, 1024), (8, SIDE)],
        gains, grad_out, sends[0], *(crossed(sends[at], at, 1) for at in (2, 3, 1)),
        scratch=[(512, SIDE)], after=[token],
    )
    grad_kernel = call(
        finish_kernel, [(4, LENGTH)], kernel_local, swapped(kernel_local, "dp", 1)
    )
    return (outputs[None], grad_inputs[None], grad_kernel, grad_skip[0], grad_mix.T, grad_conv)


def solution(mesh):
    placed = (
        P("dp", "chan", "seq"),
        P("dp", "chan", "seq"),
        P(None, "chan"),
        P(("chan", "seq"), None),
        P(("chan", "seq")),
        P(None, "chan"),
    )
    return jax.shard_map(
        shards,
        mesh=mesh,
        in_specs=placed,
        out_specs=(
            P("dp", "chan", "seq"),
            P("dp", "chan", "seq"),
            P(("chan", "seq"), None),
            P(("chan", "seq")),
            P(None, "chan"),
            P(None, "chan"),
        ),
        check_vma=False,
    )
```

```python
import functools
import math

import jax
import jax.numpy as jnp
import ml_dtypes
import numpy as np
from jax import lax
from jax.experimental import pallas as pl
from jax.experimental.pallas import tpu as pltpu
from jax.sharding import PartitionSpec as P

SIDE = 128
LENGTH = SIDE * SIDE
F32 = jnp.float32
BF16 = jnp.bfloat16
GELU_SCALE = math.sqrt(2.0 / math.pi)
GELU_CUBE = 0.044715
VMEM = pl.BlockSpec(memory_space=pltpu.VMEM)
SMEM = pl.BlockSpec(memory_space=pltpu.SMEM)
HBM = pl.BlockSpec(memory_space=pltpu.HBM)


def two_parts(table):
    high = table.astype(ml_dtypes.bfloat16)
    low = (table - high.astype(np.float64)).astype(ml_dtypes.bfloat16)
    return high, low


@functools.cache
def tables():
    one = np.arange(SIDE, dtype=np.float64)
    turn = 2.0 * np.pi * np.outer(one + 0.25, one) / SIDE
    rows = np.concatenate([np.cos(turn), -np.sin(turn)], axis=0)
    high, low = two_parts(rows)
    into_rows = np.concatenate([high, low, high], axis=1)
    high, low = two_parts(rows.T / LENGTH)
    back_rows = np.concatenate([high, low, high], axis=1)
    turn = 2.0 * np.pi * np.outer(one, one) / SIDE
    real, imag = np.cos(turn), -np.sin(turn)
    lanes = np.block([[real, imag], [-imag, real]])
    high, low = two_parts(lanes)
    into_lanes = np.concatenate([high, low, high], axis=0)
    high, low = two_parts(lanes.T)
    back_lanes = np.concatenate([high, low, high], axis=0)
    turn = 2.0 * np.pi * np.outer(one + 0.25, one) / LENGTH
    twist = np.stack([np.cos(turn), -np.sin(turn)]).astype(np.float32)
    return into_rows, into_lanes, back_rows, back_lanes, twist


def parts(value):
    high = value.astype(BF16)
    low = (value - high.astype(F32)).astype(BF16)
    return high, low


def dot(left, right, dims=((1,), (0,))):
    return lax.dot_general(left, right, (dims, ((), ())), preferred_element_type=F32)


def forward(pair, into_rows, into_lanes, twist):
    cos, sin = twist[0], twist[1]
    high, low = parts(jnp.concatenate(pair, axis=1))
    step = dot(into_rows[...], jnp.concatenate([high, high, low], axis=0))
    turned = []
    for at in range(len(pair)):
        real = step[:SIDE, at * SIDE : (at + 1) * SIDE]
        imag = step[SIDE:, at * SIDE : (at + 1) * SIDE]
        turned.append(jnp.concatenate([real * cos - imag * sin, real * sin + imag * cos], axis=1))
    high, low = parts(jnp.concatenate(turned, axis=0))
    return dot(jnp.concatenate([high, high, low], axis=1), into_lanes[...])


def backward(spectrum, back_rows, back_lanes, twist):
    cos, sin = twist[0], twist[1]
    count = spectrum.shape[0] // SIDE
    high, low = parts(spectrum)
    step = dot(jnp.concatenate([high, high, low], axis=1), back_lanes[...])
    turned = []
    for at in range(count):
        real = step[at * SIDE : (at + 1) * SIDE, :SIDE]
        imag = step[at * SIDE : (at + 1) * SIDE, SIDE:]
        turned.append(jnp.concatenate([real * cos + imag * sin, imag * cos - real * sin], axis=0))
    high, low = parts(jnp.concatenate(turned, axis=1))
    result = dot(back_rows[...], jnp.concatenate([high, high, low], axis=0))
    return [result[:, at * SIDE : (at + 1) * SIDE] for at in range(count)]


def times(left, right):
    lr, li, rr, ri = left[:, :SIDE], left[:, SIDE:], right[:, :SIDE], right[:, SIDE:]
    return jnp.concatenate([lr * rr - li * ri, lr * ri + li * rr], axis=1)


def times_conj(left, right):
    lr, li, rr, ri = left[:, :SIDE], left[:, SIDE:], right[:, :SIDE], right[:, SIDE:]
    return jnp.concatenate([lr * rr + li * ri, li * rr - lr * ri], axis=1)


def delayed(value, steps):
    row = lax.broadcasted_iota(jnp.int32, value.shape, 0)
    lane = lax.broadcasted_iota(jnp.int32, value.shape, 1)
    turned = pltpu.roll(value, steps, 1)
    above = jnp.where(row == 0, 0.0, pltpu.roll(turned, 1, 0))
    return jnp.where(lane < steps, above, turned)


def advanced(value, steps):
    row = lax.broadcasted_iota(jnp.int32, value.shape, 0)
    lane = lax.broadcasted_iota(jnp.int32, value.shape, 1)
    turned = pltpu.roll(value, SIDE - steps, 1)
    below = jnp.where(row == SIDE - 1, 0.0, pltpu.roll(turned, SIDE - 1, 0))
    return jnp.where(lane >= SIDE - steps, below, turned)


def blocks_kernel(signal, out):
    for at in range(8):
        out[pl.ds(at, 64, stride=8), :] = signal[:, at * SIDE : (at + 1) * SIDE]


def from_blocks(ref):
    return jnp.concatenate([ref[pl.ds(at, 64, stride=8), :] for at in range(8)], axis=1)


def spectrum_kernel(place_at, taps, skip, kernel, into_rows, into_lanes, twist, out, gains, rows):
    for at in range(SIDE):
        rows[pl.ds(at, 4, stride=SIDE), :] = kernel[:, at * SIDE : (at + 1) * SIDE]
    line = lax.broadcasted_iota(jnp.int32, (SIDE, SIDE), 0)
    lane = lax.broadcasted_iota(jnp.int32, (SIDE, SIDE), 1)
    start = (line == 0) & (lane == 0)
    every = [
        rows[at * SIDE : (at + 1) * SIDE, :] + jnp.where(start, skip[at], 0.0) for at in range(4)
    ]
    out[...] = forward(every, into_rows, into_lanes, twist)
    line, lane = line[:16], lane[:16]
    first, chan = 4 * place_at[0], place_at[1]
    result = jnp.where(line == 3, jnp.bitwise_and(chan, 1).astype(F32), 0.0)
    result = jnp.where(line == 4, lax.shift_right_logical(chan, 1).astype(F32), result)
    turn = 2 * jnp.bitwise_and(chan, 1)
    for row, bit in ((5, 2), (6, 3), (7, 0), (12, 1)):
        bit = bit + turn if bit < 2 else bit - turn
        one = jnp.bitwise_and(lax.shift_right_logical(place_at[0], bit), 1)
        result = jnp.where(line == row, one.astype(F32), result)
    result = jnp.where((line >= 8) & (line < 12) & (lane == first + line - 8), 1.0, result)
    for tap in range(3):
        for at in range(4):
            result = jnp.where((line == tap) & (lane == at), taps[tap, first + at], result)
    gains[...] = result


def weights_kernel(place_at, mix, mix_far, _rows, _lanes, into, back):
    chan = place_at[1]
    start = pl.multiple_of(128 * lax.shift_right_logical(chan, 1), 128)
    both = jnp.concatenate([mix[:, pl.ds(start, 128)], mix_far[...]], axis=0)
    both = pltpu.roll(both, 64 * jnp.bitwise_and(chan, 1), 1)
    high, low = parts(both)
    back[...] = jnp.concatenate([high, low, high], axis=1)
    high, low = parts(both.T)
    into[...] = jnp.concatenate([high, low, high], axis=1)


def grad_act_kernel(cot, cot_far, weights, own, other):
    for half in range(4):
        lanes = slice(half * 256, (half + 1) * 256)
        high, low = parts(jnp.concatenate([cot[:, lanes], cot_far[:, lanes]], axis=0))
        result = dot(weights[...], jnp.concatenate([high, high, low], axis=0))
        for at in range(2):
            place = pl.ds(2 * half + at, 64, stride=8)
            own[place, :] = result[:64, at * SIDE : (at + 1) * SIDE]
            other[place, :] = result[64:, at * SIDE : (at + 1) * SIDE]


def channel(ref, at):
    return ref[:, at * 8 : (at + 1) * 8, :].reshape(SIDE, SIDE)


def gains_of(gains, at):
    return [jnp.broadcast_to(gains[tap : tap + 1, at : at + 1], (SIDE, SIDE)) for tap in range(3)]


def moved(copies):
    for one in copies:
        one.start()
    return copies


def forward_kernel(
    gains, signal, kernel_spec, into_rows, into_lanes, back_rows, back_lanes, twist,
    spec, long_conv, slopes, act_out, act, sem,
):
    spectrum = forward([channel(signal, at) for at in range(4)], into_rows, into_lanes, twist)
    spec[...] = spectrum
    result = backward(times(spectrum, kernel_spec[...]), back_rows, back_lanes, twist)
    for index in range(4):
        taps = gains_of(gains, index)
        whole = result[index]
        long_conv[index] = whole
        value = taps[2] * whole + taps[1] * delayed(whole, 1) + taps[0] * delayed(whole, 2)
        square = value * value
        half = 0.5 + 0.5 * jnp.tanh(value * (GELU_SCALE + GELU_SCALE * GELU_CUBE * square))
        act[:, index * 8 : (index + 1) * 8, :] = (value * half).reshape(16, 8, SIDE)
        slopes[index] = half + half * (1.0 - half) * value * (
            2.0 * GELU_SCALE + 6.0 * GELU_SCALE * GELU_CUBE * square
        )
    copy = pltpu.make_async_copy(act, act_out.at[:, pl.ds(0, 32), :], sem)
    copy.start()
    copy.wait()


def join_kernel(act, own, near, out, total, sem):
    total[...] = (own[...] + near[...]).reshape(16, 32, SIDE)
    copy = pltpu.make_async_copy(total, out.at[:, pl.ds(32, 32), :], sem)
    copy.start()
    copy.wait()


def slope_kernel(
    gains, grad_act, signal, long_conv, slopes, into_rows, into_lanes, twist, grad_spec, small,
):
    small[...] = jnp.zeros_like(small)
    grads = []
    for index in range(4):
        taps = gains_of(gains, index)
        grad = channel(grad_act, 4 + index) * slopes[index]
        later = [advanced(grad, 2), advanced(grad, 1), grad]
        grads.append(taps[0] * later[0] + taps[1] * later[1] + taps[2] * later[2])
        pairs = [one * long_conv[index] for one in later] + [grads[index] * channel(signal, index)]
        sums = jnp.concatenate([jnp.sum(one, axis=0, keepdims=True) for one in pairs], axis=0)
        small[:4, :] = small[:4, :] + jnp.sum(sums, axis=1, keepdims=True) * gains[8 + index : 9 + index, :]
    grad_spec[...] = forward(grads, into_rows, into_lanes, twist)


def backward_kernel(
    grad_spec, spec, kernel_spec, back_rows, back_lanes, twist,
    grad_in, kernel_out, rows,
):
    spectrum = grad_spec[...]
    result = backward(times_conj(spectrum, kernel_spec[...]), back_rows, back_lanes, twist)
    for at in range(4):
        grad_in[:, at * 8 : (at + 1) * 8, :] = result[at].reshape(16, 8, SIDE)
    result = backward(times_conj(spectrum, spec[...]), back_rows, back_lanes, twist)
    for at in range(4):
        rows[at * SIDE : (at + 1) * SIDE, :] = result[at]
    for at in range(SIDE):
        kernel_out[:, at * SIDE : (at + 1) * SIDE] = rows[pl.ds(at, 4, stride=SIDE), :]


def tail_kernel(act, act_near, cot, cot_far, signal, weights, small, mine, theirs, out, out_far):
    active = jnp.concatenate([from_blocks(act), from_blocks(act_near)], axis=0)
    act_high, act_low = parts(active)
    high, low = parts(jnp.concatenate([cot[...], cot_far[...]], axis=0))
    result = dot(
        jnp.concatenate([high, low, high], axis=1),
        jnp.concatenate([act_high, act_high, act_low], axis=1),
        ((1,), (1,)),
    )
    mine[:64, :] = result[:64]
    mine[64:, :] = small[...]
    theirs[...] = result[64:]
    mixed = dot(weights[...], jnp.concatenate([act_high, act_high, act_low], axis=0))
    out[...] = signal[...] + mixed[:64]
    out_far[...] = mixed[64:]


def flag(gains, row, shape):
    return jnp.broadcast_to(gains[row : row + 1, :], shape) > 0.5


def relative(blocks, low, high):
    blocks = [jnp.where(low, blocks[at ^ 1], blocks[at]) for at in range(4)]
    return [jnp.where(high, blocks[at ^ 2], blocks[at]) for at in range(4)]


def by_core(grid, swap):
    return [[jnp.where(swap, grid[b][a], grid[a][b]) if a != b else grid[a][a] for b in range(4)] for a in range(4)]


def merge_kernel(gains, grad, mine, mine_far, theirs_far, theirs, out0, out1, out2, out3):
    total = [
        mine[:64, :] + mine_far[:64, :],
        theirs[...] + theirs_far[...],
        mine[64:, :] + mine_far[64:, :],
    ]
    shape = (SIDE, SIDE)
    grid = by_core([[grad[4 * a + b] for b in range(4)] for a in range(4)], flag(gains, 3, (32, SIDE)))
    blocks = relative([jnp.concatenate(row, axis=0) for row in grid], flag(gains, 5, shape), flag(gains, 6, shape))
    for out, block in zip((out0, out1, out2, out3), blocks):
        out[:64, :] = total[0]
        out[64:128, :] = total[1]
        out[128:136, :] = total[2]
        out[136:, :] = block


def sum_kernel(gains, in0, in2, in3, in1, out0, out1, out2, out3):
    whole = in0[:136, :] + in1[:136, :] + in2[:136, :] + in3[:136, :]
    outs = (out0, out1, out2, out3)
    for out in outs:
        out[:136, :] = whole
    shape = (32, SIDE)
    low, high = flag(gains, 7, shape), flag(gains, 12, shape)
    for near, ref in enumerate((in0, in1, in2, in3)):
        blocks = relative([ref[136 + 32 * at : 168 + 32 * at, :] for at in range(4)], low, high)
        for out, block in zip(outs, blocks):
            out[136 + 32 * near : 168 + 32 * near, :] = block


def outputs_kernel(own, near, outputs, token):
    outputs[...] = own[...] + near[...]
    token[...] = jnp.zeros_like(token)


def finish_kernel(own, near, grad_kernel):
    grad_kernel[...] = own[...] + near[...]


def final_kernel(gains, cotangent, in0, in2, in3, in1, out, taps, skip, grad_inputs, token, rows):
    core, place = flag(gains, 3, (64, SIDE)), flag(gains, 4, (64, SIDE))
    whole = in0[:136, :] + in1[:136, :] + in2[:136, :] + in3[:136, :]
    near, far = [
        jnp.where(core, pltpu.roll(one, 64, 1), one) for one in (whole[:64], whole[64:128])
    ]
    out[:, :SIDE] = jnp.where(place, far, near)
    out[:, SIDE:] = jnp.where(place, near, far)
    token[...] = jnp.zeros_like(token)
    taps[...] = whole[128:131, :64]
    own = jnp.sum(whole[131:132] * gains[8:12, :], axis=1, keepdims=True)
    line = lax.broadcasted_iota(jnp.int32, (4, SIDE), 0)
    lane = lax.broadcasted_iota(jnp.int32, (4, SIDE), 1)
    skip[...] = jnp.sum(jnp.where(line == lane, own, 0.0), axis=0, keepdims=True)[:, :4]
    shape = (SIDE, SIDE)
    columns = relative([ref[136:, :] for ref in (in0, in1, in2, in3)], flag(gains, 7, shape), flag(gains, 12, shape))
    shape = (32, SIDE)
    low, high = flag(gains, 5, shape), flag(gains, 6, shape)
    columns = [relative([column[32 * at : 32 * at + 32] for at in range(4)], low, high) for column in columns]
    grid = by_core([[columns[b][a] for b in range(4)] for a in range(4)], flag(gains, 3, shape))
    for z in range(4):
        for x in range(4):
            rows[(4 * z + x) * 32 : (4 * z + x + 1) * 32, :] = grid[z][x]
    for at in range(8):
        lanes = slice(at * SIDE, (at + 1) * SIDE)
        grad_inputs[:, lanes] = cotangent[:, lanes] + rows[pl.ds(at, 64, stride=8), :]


def call(kernel, outs, *args, scalars=0, far=(), far_outs=(), scratch=(), after=(), aliases=()):
    shapes = [shape if not isinstance(shape, tuple) else jax.ShapeDtypeStruct(shape, F32) for shape in outs]
    count = len(args)

    def body(*refs):
        kernel(*refs[:count], *refs[count + len(after) :])

    ins = [SMEM if at < scalars else HBM if at in far else VMEM for at in range(count)]
    places = [HBM if at in far_outs else VMEM for at in range(len(outs))]
    return pl.pallas_call(
        body,
        out_shape=shapes if len(shapes) > 1 else shapes[0],
        in_specs=ins + [pl.BlockSpec(memory_space=pl.ANY)] * len(after),
        out_specs=places if len(shapes) > 1 else places[0],
        scratch_shapes=[shape if not isinstance(shape, tuple) else pltpu.VMEM(shape, F32) for shape in scratch],
        compiler_params=pltpu.CompilerParams(vmem_limit_bytes=20 * 1024 * 1024),
        input_output_aliases=dict(aliases),
        name=kernel.__name__,
        cost_estimate=pl.CostEstimate(flops=20000000000, bytes_accessed=0, transcendentals=0) if kernel is forward_kernel else None,
    )(*args, *after)


def swapped(value, axes, flip):
    count = lax.axis_size(axes)
    return lax.ppermute(value, axes, [(at, at ^ flip) for at in range(count)])


def crossed(value, flip, second):
    pairs = []
    for seq in range(16):
        for chan in range(4):
            there = seq ^ (flip if (chan + second) % 2 else 4 * flip)
            pairs.append((4 * seq + chan, 4 * there + chan))
    return lax.ppermute(value, ("seq", "chan"), pairs)


def turned(value):
    return lax.all_to_all(value, "seq", 0, 0, tiled=True)


def shards(inputs, cotangent, conv_weight, kernel, skip_gain, mix_weight):
    signal = inputs[0]
    grad_out = cotangent[0]
    seq, chan = lax.axis_index("seq"), lax.axis_index("chan")
    place_at = jnp.stack([seq, chan]).astype(jnp.int32)
    into_rows, into_lanes, back_rows, back_lanes, twist = (jnp.asarray(table) for table in tables())
    mix = mix_weight.T

    cot_far = swapped(grad_out, "chan", 2)
    far = jnp.bitwise_xor(lax.shift_right_logical(chan, 1), 1)
    mix_far = swapped(lax.dynamic_slice(mix, (0, 128 * far), (64, 128)), "chan", 2)
    signal_blocks = call(
        blocks_kernel, [(512, SIDE)], signal
    )
    signal_in = turned(signal_blocks.reshape(16, 32, SIDE))
    kernel_spec, gains = call(
        spectrum_kernel, [(512, 256), (16, SIDE)],
        place_at, conv_weight, skip_gain, kernel, into_rows, into_lanes, twist,
        scalars=3, scratch=[(512, SIDE)], after=[signal_blocks],
    )
    weights_into, weights_back = call(
        weights_kernel, [jax.ShapeDtypeStruct((SIDE, 3 * SIDE), BF16)] * 2, place_at, mix, mix_far,
        back_rows, back_lanes, scalars=1,
    )
    grad_own, grad_other = call(
        grad_act_kernel, [(512, SIDE)] * 2, grad_out, cot_far, weights_into
    )
    grad_near = swapped(grad_other, "chan", 1)
    spec, long_conv, slopes, act = call(
        forward_kernel,
        [(512, 256), (4, SIDE, SIDE), (4, SIDE, SIDE), (16, 64, SIDE)],
        gains, signal_in, kernel_spec, into_rows, into_lanes, back_rows, back_lanes, twist,
        far_outs=(3,), after=[grad_own], scratch=[(16, 32, SIDE), pltpu.SemaphoreType.DMA],
    )
    act = call(
        join_kernel, [(16, 64, SIDE)], act, grad_own, grad_near,
        far=(0,), far_outs=(0,), aliases={0: 0}, scratch=[(16, 32, SIDE), pltpu.SemaphoreType.DMA],
    )
    act_in = turned(act)
    act_own = act_in[:, :32].reshape(512, SIDE)
    act_near = swapped(act_own, "chan", 1)
    grad_spec, small = call(
        slope_kernel, [(512, 256), (8, SIDE)], gains, act_in, signal_in, long_conv, slopes, into_rows, into_lanes, twist
    )
    mine, theirs, out_own, out_far = call(
        tail_kernel,
        [(72, SIDE), (64, SIDE), (64, 1024), (64, 1024)],
        act_own, act_near, grad_out, cot_far, signal, weights_back, small,
    )
    grad_long, kernel_local = call(
        backward_kernel,
        [(16, 32, SIDE), (4, LENGTH)],
        grad_spec, spec, kernel_spec, back_rows, back_lanes, twist,
        after=[mine], scratch=[(512, SIDE)],
    )
    both = ("dp", "chan")
    far_theirs = [swapped(theirs, both, flip) for flip in (6, 2)]
    sends = call(
        merge_kernel, [(264, SIDE)] * 4, gains, grad_long, mine, swapped(mine, both, 4), *far_theirs
    )
    sends = call(
        sum_kernel, [(264, SIDE)] * 4,
        gains, sends[0], *(crossed(sends[at], at, 0) for at in (2, 3, 1)),
    )
    outputs, token = call(
        outputs_kernel, [(64, 1024), (8, SIDE)], out_own, swapped(out_far, "chan", 2)
    )
    grad_mix, grad_conv, grad_skip, grad_inputs, token = call(
        final_kernel, [(64, 256), (3, 64), (1, 4), (64, 1024), (8, SIDE)],
        gains, grad_out, sends[0], *(crossed(sends[at], at, 1) for at in (2, 3, 1)),
        scratch=[(512, SIDE)], after=[token],
    )
    grad_kernel = call(
        finish_kernel, [(4, LENGTH)], kernel_local, swapped(kernel_local, "dp", 1)
    )
    return (outputs[None], grad_inputs[None], grad_kernel, grad_skip[0], grad_mix.T, grad_conv)


def solution(mesh):
    placed = (
        P("dp", "chan", "seq"),
        P("dp", "chan", "seq"),
        P(None, "chan"),
        P(("chan", "seq"), None),
        P(("chan", "seq")),
        P(None, "chan"),
    )
    return jax.shard_map(
        shards,
        mesh=mesh,
        in_specs=placed,
        out_specs=(
            P("dp", "chan", "seq"),
            P("dp", "chan", "seq"),
            P(("chan", "seq"), None),
            P(("chan", "seq")),
            P(None, "chan"),
            P(None, "chan"),
        ),
        check_vma=False,
    )
```

```python
import functools
import math

import jax
import jax.numpy as jnp
import ml_dtypes
import numpy as np
from jax import lax
from jax.experimental import pallas as pl
from jax.experimental.pallas import tpu as pltpu
from jax.sharding import PartitionSpec as P

SIDE = 128
LENGTH = SIDE * SIDE
F32 = jnp.float32
BF16 = jnp.bfloat16
GELU_SCALE = math.sqrt(2.0 / math.pi)
GELU_CUBE = 0.044715
VMEM = pl.BlockSpec(memory_space=pltpu.VMEM)
SMEM = pl.BlockSpec(memory_space=pltpu.SMEM)
HBM = pl.BlockSpec(memory_space=pltpu.HBM)


def two_parts(table):
    high = table.astype(ml_dtypes.bfloat16)
    low = (table - high.astype(np.float64)).astype(ml_dtypes.bfloat16)
    return high, low


@functools.cache
def tables():
    one = np.arange(SIDE, dtype=np.float64)
    turn = 2.0 * np.pi * np.outer(one + 0.25, one) / SIDE
    rows = np.concatenate([np.cos(turn), -np.sin(turn)], axis=0)
    high, low = two_parts(rows)
    into_rows = np.concatenate([high, low, high], axis=1)
    high, low = two_parts(rows.T / LENGTH)
    back_rows = np.concatenate([high, low, high], axis=1)
    turn = 2.0 * np.pi * np.outer(one, one) / SIDE
    real, imag = np.cos(turn), -np.sin(turn)
    lanes = np.block([[real, imag], [-imag, real]])
    high, low = two_parts(lanes)
    into_lanes = np.concatenate([high, low, high], axis=0)
    high, low = two_parts(lanes.T)
    back_lanes = np.concatenate([high, low, high], axis=0)
    turn = 2.0 * np.pi * np.outer(one + 0.25, one) / LENGTH
    twist = np.stack([np.cos(turn), -np.sin(turn)]).astype(np.float32)
    return into_rows, into_lanes, back_rows, back_lanes, twist


def parts(value):
    high = value.astype(BF16)
    low = (value - high.astype(F32)).astype(BF16)
    return high, low


def dot(left, right, dims=((1,), (0,))):
    return lax.dot_general(left, right, (dims, ((), ())), preferred_element_type=F32)


def forward(pair, into_rows, into_lanes, twist):
    cos, sin = twist[0], twist[1]
    high, low = parts(jnp.concatenate(pair, axis=1))
    step = dot(into_rows[...], jnp.concatenate([high, high, low], axis=0))
    turned = []
    for at in range(len(pair)):
        real = step[:SIDE, at * SIDE : (at + 1) * SIDE]
        imag = step[SIDE:, at * SIDE : (at + 1) * SIDE]
        turned.append(jnp.concatenate([real * cos - imag * sin, real * sin + imag * cos], axis=1))
    high, low = parts(jnp.concatenate(turned, axis=0))
    return dot(jnp.concatenate([high, high, low], axis=1), into_lanes[...])


def backward(spectrum, back_rows, back_lanes, twist):
    cos, sin = twist[0], twist[1]
    count = spectrum.shape[0] // SIDE
    high, low = parts(spectrum)
    step = dot(jnp.concatenate([high, high, low], axis=1), back_lanes[...])
    turned = []
    for at in range(count):
        real = step[at * SIDE : (at + 1) * SIDE, :SIDE]
        imag = step[at * SIDE : (at + 1) * SIDE, SIDE:]
        turned.append(jnp.concatenate([real * cos + imag * sin, imag * cos - real * sin], axis=0))
    high, low = parts(jnp.concatenate(turned, axis=1))
    result = dot(back_rows[...], jnp.concatenate([high, high, low], axis=0))
    return [result[:, at * SIDE : (at + 1) * SIDE] for at in range(count)]


def times(left, right):
    lr, li, rr, ri = left[:, :SIDE], left[:, SIDE:], right[:, :SIDE], right[:, SIDE:]
    return jnp.concatenate([lr * rr - li * ri, lr * ri + li * rr], axis=1)


def times_conj(left, right):
    lr, li, rr, ri = left[:, :SIDE], left[:, SIDE:], right[:, :SIDE], right[:, SIDE:]
    return jnp.concatenate([lr * rr + li * ri, li * rr - lr * ri], axis=1)


def delayed(value, steps):
    row = lax.broadcasted_iota(jnp.int32, value.shape, 0)
    lane = lax.broadcasted_iota(jnp.int32, value.shape, 1)
    turned = pltpu.roll(value, steps, 1)
    above = jnp.where(row == 0, 0.0, pltpu.roll(turned, 1, 0))
    return jnp.where(lane < steps, above, turned)


def advanced(value, steps):
    row = lax.broadcasted_iota(jnp.int32, value.shape, 0)
    lane = lax.broadcasted_iota(jnp.int32, value.shape, 1)
    turned = pltpu.roll(value, SIDE - steps, 1)
    below = jnp.where(row == SIDE - 1, 0.0, pltpu.roll(turned, SIDE - 1, 0))
    return jnp.where(lane >= SIDE - steps, below, turned)


def blocks_kernel(signal, out):
    for at in range(8):
        out[pl.ds(at, 64, stride=8), :] = signal[:, at * SIDE : (at + 1) * SIDE]


def from_blocks(ref):
    return jnp.concatenate([ref[pl.ds(at, 64, stride=8), :] for at in range(8)], axis=1)


def spectrum_kernel(place_at, taps, skip, kernel, into_rows, into_lanes, twist, out, gains, rows):
    for at in range(SIDE):
        rows[pl.ds(at, 4, stride=SIDE), :] = kernel[:, at * SIDE : (at + 1) * SIDE]
    line = lax.broadcasted_iota(jnp.int32, (SIDE, SIDE), 0)
    lane = lax.broadcasted_iota(jnp.int32, (SIDE, SIDE), 1)
    start = (line == 0) & (lane == 0)
    every = [
        rows[at * SIDE : (at + 1) * SIDE, :] + jnp.where(start, skip[at], 0.0) for at in range(4)
    ]
    out[...] = forward(every, into_rows, into_lanes, twist)
    line, lane = line[:16], lane[:16]
    first, chan = 4 * place_at[0], place_at[1]
    result = jnp.where(line == 3, jnp.bitwise_and(chan, 1).astype(F32), 0.0)
    result = jnp.where(line == 4, lax.shift_right_logical(chan, 1).astype(F32), result)
    turn = 2 * jnp.bitwise_and(chan, 1)
    for row, bit in ((5, 2), (6, 3), (7, 0), (12, 1)):
        bit = bit + turn if bit < 2 else bit - turn
        one = jnp.bitwise_and(lax.shift_right_logical(place_at[0], bit), 1)
        result = jnp.where(line == row, one.astype(F32), result)
    result = jnp.where((line >= 8) & (line < 12) & (lane == first + line - 8), 1.0, result)
    for tap in range(3):
        for at in range(4):
            result = jnp.where((line == tap) & (lane == at), taps[tap, first + at], result)
    gains[...] = result


def weights_kernel(place_at, mix, mix_far, _rows, _lanes, into, back):
    chan = place_at[1]
    start = pl.multiple_of(128 * lax.shift_right_logical(chan, 1), 128)
    both = jnp.concatenate([mix[:, pl.ds(start, 128)], mix_far[:, pl.ds(start, 128)]], axis=0)
    both = pltpu.roll(both, 64 * jnp.bitwise_and(chan, 1), 1)
    high, low = parts(both)
    back[...] = jnp.concatenate([high, low, high], axis=1)
    high, low = parts(both.T)
    into[...] = jnp.concatenate([high, low, high], axis=1)


def grad_act_kernel(cot, cot_far, weights, own, other):
    for half in range(4):
        lanes = slice(half * 256, (half + 1) * 256)
        high, low = parts(jnp.concatenate([cot[:, lanes], cot_far[:, lanes]], axis=0))
        result = dot(weights[...], jnp.concatenate([high, high, low], axis=0))
        for at in range(2):
            place = pl.ds(2 * half + at, 64, stride=8)
            own[place, :] = result[:64, at * SIDE : (at + 1) * SIDE]
            other[place, :] = result[64:, at * SIDE : (at + 1) * SIDE]


def channel(ref, at):
    return ref[:, at * 8 : (at + 1) * 8, :].reshape(SIDE, SIDE)


def gains_of(gains, at):
    return [jnp.broadcast_to(gains[tap : tap + 1, at : at + 1], (SIDE, SIDE)) for tap in range(3)]


def moved(copies):
    for one in copies:
        one.start()
    return copies


def forward_kernel(
    gains, signal, kernel_spec, into_rows, into_lanes, back_rows, back_lanes, twist,
    spec, long_conv, slopes, act_out, act, sem,
):
    spectrum = forward([channel(signal, at) for at in range(4)], into_rows, into_lanes, twist)
    spec[...] = spectrum
    result = backward(times(spectrum, kernel_spec[...]), back_rows, back_lanes, twist)
    for index in range(4):
        taps = gains_of(gains, index)
        whole = result[index]
        long_conv[index] = whole
        value = taps[2] * whole + taps[1] * delayed(whole, 1) + taps[0] * delayed(whole, 2)
        square = value * value
        half = 0.5 + 0.5 * jnp.tanh(value * (GELU_SCALE + GELU_SCALE * GELU_CUBE * square))
        act[:, index * 8 : (index + 1) * 8, :] = (value * half).reshape(16, 8, SIDE)
        slopes[index] = half + half * (1.0 - half) * value * (
            2.0 * GELU_SCALE + 6.0 * GELU_SCALE * GELU_CUBE * square
        )
    copy = pltpu.make_async_copy(act, act_out.at[:, pl.ds(0, 32), :], sem)
    copy.start()
    copy.wait()


def join_kernel(act, own, near, out, total, sem):
    total[...] = (own[...] + near[...]).reshape(16, 32, SIDE)
    copy = pltpu.make_async_copy(total, out.at[:, pl.ds(32, 32), :], sem)
    copy.start()
    copy.wait()


def slope_kernel(
    gains, grad_act, signal, long_conv, slopes, into_rows, into_lanes, twist, grad_spec, small,
):
    small[...] = jnp.zeros_like(small)
    grads = []
    for index in range(4):
        taps = gains_of(gains, index)
        grad = channel(grad_act, 4 + index) * slopes[index]
        later = [advanced(grad, 2), advanced(grad, 1), grad]
        grads.append(taps[0] * later[0] + taps[1] * later[1] + taps[2] * later[2])
        pairs = [one * long_conv[index] for one in later] + [grads[index] * channel(signal, index)]
        sums = jnp.concatenate([jnp.sum(one, axis=0, keepdims=True) for one in pairs], axis=0)
        small[:4, :] = small[:4, :] + jnp.sum(sums, axis=1, keepdims=True) * gains[8 + index : 9 + index, :]
    grad_spec[...] = forward(grads, into_rows, into_lanes, twist)


def backward_kernel(
    grad_spec, spec, kernel_spec, back_rows, back_lanes, twist,
    grad_in, kernel_out, rows,
):
    spectrum = grad_spec[...]
    result = backward(times_conj(spectrum, kernel_spec[...]), back_rows, back_lanes, twist)
    for at in range(4):
        grad_in[:, at * 8 : (at + 1) * 8, :] = result[at].reshape(16, 8, SIDE)
    result = backward(times_conj(spectrum, spec[...]), back_rows, back_lanes, twist)
    for at in range(4):
        rows[at * SIDE : (at + 1) * SIDE, :] = result[at]
    for at in range(SIDE):
        kernel_out[:, at * SIDE : (at + 1) * SIDE] = rows[pl.ds(at, 4, stride=SIDE), :]


def tail_kernel(act, act_near, cot, cot_far, signal, weights, small, mine, theirs, out, out_far):
    active = jnp.concatenate([from_blocks(act), from_blocks(act_near)], axis=0)
    act_high, act_low = parts(active)
    high, low = parts(jnp.concatenate([cot[...], cot_far[...]], axis=0))
    result = dot(
        jnp.concatenate([high, low, high], axis=1),
        jnp.concatenate([act_high, act_high, act_low], axis=1),
        ((1,), (1,)),
    )
    mine[:64, :] = result[:64]
    mine[64:, :] = small[...]
    theirs[...] = result[64:]
    mixed = dot(weights[...], jnp.concatenate([act_high, act_high, act_low], axis=0))
    out[...] = signal[...] + mixed[:64]
    out_far[...] = mixed[64:]


def flag(gains, row, shape):
    return jnp.broadcast_to(gains[row : row + 1, :], shape) > 0.5


def relative(blocks, low, high):
    blocks = [jnp.where(low, blocks[at ^ 1], blocks[at]) for at in range(4)]
    return [jnp.where(high, blocks[at ^ 2], blocks[at]) for at in range(4)]


def by_core(grid, swap):
    return [[jnp.where(swap, grid[b][a], grid[a][b]) if a != b else grid[a][a] for b in range(4)] for a in range(4)]


def merge_kernel(gains, grad, mine, mine_far, theirs_far, theirs, out0, out1, out2, out3):
    total = [
        mine[:64, :] + mine_far[:64, :],
        theirs[...] + theirs_far[...],
        mine[64:, :] + mine_far[64:, :],
    ]
    shape = (SIDE, SIDE)
    grid = by_core([[grad[4 * a + b] for b in range(4)] for a in range(4)], flag(gains, 3, (32, SIDE)))
    blocks = relative([jnp.concatenate(row, axis=0) for row in grid], flag(gains, 5, shape), flag(gains, 6, shape))
    for out, block in zip((out0, out1, out2, out3), blocks):
        out[:64, :] = total[0]
        out[64:128, :] = total[1]
        out[128:136, :] = total[2]
        out[136:, :] = block


def sum_kernel(gains, in0, in2, in3, in1, out0, out1, out2, out3):
    whole = in0[:136, :] + in1[:136, :] + in2[:136, :] + in3[:136, :]
    outs = (out0, out1, out2, out3)
    for out in outs:
        out[:136, :] = whole
    shape = (32, SIDE)
    low, high = flag(gains, 7, shape), flag(gains, 12, shape)
    for near, ref in enumerate((in0, in1, in2, in3)):
        blocks = relative([ref[136 + 32 * at : 168 + 32 * at, :] for at in range(4)], low, high)
        for out, block in zip(outs, blocks):
            out[136 + 32 * near : 168 + 32 * near, :] = block


def outputs_kernel(own, near, outputs, token):
    outputs[...] = own[...] + near[...]
    token[...] = jnp.zeros_like(token)


def finish_kernel(own, near, grad_kernel):
    grad_kernel[...] = own[...] + near[...]


def final_kernel(gains, cotangent, in0, in2, in3, in1, out, taps, skip, grad_inputs, token, rows):
    core, place = flag(gains, 3, (64, SIDE)), flag(gains, 4, (64, SIDE))
    whole = in0[:136, :] + in1[:136, :] + in2[:136, :] + in3[:136, :]
    near, far = [
        jnp.where(core, pltpu.roll(one, 64, 1), one) for one in (whole[:64], whole[64:128])
    ]
    out[:, :SIDE] = jnp.where(place, far, near)
    out[:, SIDE:] = jnp.where(place, near, far)
    token[...] = jnp.zeros_like(token)
    taps[...] = whole[128:131, :64]
    own = jnp.sum(whole[131:132] * gains[8:12, :], axis=1, keepdims=True)
    line = lax.broadcasted_iota(jnp.int32, (4, SIDE), 0)
    lane = lax.broadcasted_iota(jnp.int32, (4, SIDE), 1)
    skip[...] = jnp.sum(jnp.where(line == lane, own, 0.0), axis=0, keepdims=True)[:, :4]
    shape = (SIDE, SIDE)
    columns = relative([ref[136:, :] for ref in (in0, in1, in2, in3)], flag(gains, 7, shape), flag(gains, 12, shape))
    shape = (32, SIDE)
    low, high = flag(gains, 5, shape), flag(gains, 6, shape)
    columns = [relative([column[32 * at : 32 * at + 32] for at in range(4)], low, high) for column in columns]
    grid = by_core([[columns[b][a] for b in range(4)] for a in range(4)], flag(gains, 3, shape))
    for z in range(4):
        for x in range(4):
            rows[(4 * z + x) * 32 : (4 * z + x + 1) * 32, :] = grid[z][x]
    for at in range(8):
        lanes = slice(at * SIDE, (at + 1) * SIDE)
        grad_inputs[:, lanes] = cotangent[:, lanes] + rows[pl.ds(at, 64, stride=8), :]


def call(kernel, outs, *args, scalars=0, far=(), far_outs=(), scratch=(), after=(), aliases=()):
    shapes = [shape if not isinstance(shape, tuple) else jax.ShapeDtypeStruct(shape, F32) for shape in outs]
    count = len(args)

    def body(*refs):
        kernel(*refs[:count], *refs[count + len(after) :])

    ins = [SMEM if at < scalars else HBM if at in far else VMEM for at in range(count)]
    places = [HBM if at in far_outs else VMEM for at in range(len(outs))]
    return pl.pallas_call(
        body,
        out_shape=shapes if len(shapes) > 1 else shapes[0],
        in_specs=ins + [pl.BlockSpec(memory_space=pl.ANY)] * len(after),
        out_specs=places if len(shapes) > 1 else places[0],
        scratch_shapes=[shape if not isinstance(shape, tuple) else pltpu.VMEM(shape, F32) for shape in scratch],
        compiler_params=pltpu.CompilerParams(vmem_limit_bytes=20 * 1024 * 1024),
        input_output_aliases=dict(aliases),
        name=kernel.__name__,
        cost_estimate=pl.CostEstimate(flops=20000000000, bytes_accessed=0, transcendentals=0) if kernel in (forward_kernel, grad_act_kernel) else None,
    )(*args, *after)


def swapped(value, axes, flip):
    count = lax.axis_size(axes)
    return lax.ppermute(value, axes, [(at, at ^ flip) for at in range(count)])


def crossed(value, flip, second):
    pairs = []
    for seq in range(16):
        for chan in range(4):
            there = seq ^ (flip if (chan + second) % 2 else 4 * flip)
            pairs.append((4 * seq + chan, 4 * there + chan))
    return lax.ppermute(value, ("seq", "chan"), pairs)


def turned(value):
    return lax.all_to_all(value, "seq", 0, 0, tiled=True)


def shards(inputs, cotangent, conv_weight, kernel, skip_gain, mix_weight):
    signal = inputs[0]
    grad_out = cotangent[0]
    seq, chan = lax.axis_index("seq"), lax.axis_index("chan")
    place_at = jnp.stack([seq, chan]).astype(jnp.int32)
    into_rows, into_lanes, back_rows, back_lanes, twist = (jnp.asarray(table) for table in tables())
    mix = mix_weight.T

    cot_far = swapped(grad_out, "chan", 2)
    mix_far = swapped(mix, "chan", 2)
    signal_blocks = call(
        blocks_kernel, [(512, SIDE)], signal
    )
    signal_in = turned(signal_blocks.reshape(16, 32, SIDE))
    kernel_spec, gains = call(
        spectrum_kernel, [(512, 256), (16, SIDE)],
        place_at, conv_weight, skip_gain, kernel, into_rows, into_lanes, twist,
        scalars=3, scratch=[(512, SIDE)], after=[signal_blocks],
    )
    weights_into, weights_back = call(
        weights_kernel, [jax.ShapeDtypeStruct((SIDE, 3 * SIDE), BF16)] * 2, place_at, mix, mix_far,
        back_rows, back_lanes, scalars=1,
    )
    grad_own, grad_other = call(
        grad_act_kernel, [(512, SIDE)] * 2, grad_out, cot_far, weights_into
    )
    grad_near = swapped(grad_other, "chan", 1)
    spec, long_conv, slopes, act = call(
        forward_kernel,
        [(512, 256), (4, SIDE, SIDE), (4, SIDE, SIDE), (16, 64, SIDE)],
        gains, signal_in, kernel_spec, into_rows, into_lanes, back_rows, back_lanes, twist,
        far_outs=(3,), after=[grad_own], scratch=[(16, 32, SIDE), pltpu.SemaphoreType.DMA],
    )
    act = call(
        join_kernel, [(16, 64, SIDE)], act, grad_own, grad_near,
        far=(0,), far_outs=(0,), aliases={0: 0}, scratch=[(16, 32, SIDE), pltpu.SemaphoreType.DMA],
    )
    act_in = turned(act)
    act_own = act_in[:, :32].reshape(512, SIDE)
    act_near = swapped(act_own, "chan", 1)
    grad_spec, small = call(
        slope_kernel, [(512, 256), (8, SIDE)], gains, act_in, signal_in, long_conv, slopes, into_rows, into_lanes, twist
    )
    mine, theirs, out_own, out_far = call(
        tail_kernel,
        [(72, SIDE), (64, SIDE), (64, 1024), (64, 1024)],
        act_own, act_near, grad_out, cot_far, signal, weights_back, small,
    )
    grad_long, kernel_local = call(
        backward_kernel,
        [(16, 32, SIDE), (4, LENGTH)],
        grad_spec, spec, kernel_spec, back_rows, back_lanes, twist,
        after=[mine], scratch=[(512, SIDE)],
    )
    both = ("dp", "chan")
    far_theirs = [swapped(theirs, both, flip) for flip in (6, 2)]
    sends = call(
        merge_kernel, [(264, SIDE)] * 4, gains, grad_long, mine, swapped(mine, both, 4), *far_theirs
    )
    sends = call(
        sum_kernel, [(264, SIDE)] * 4,
        gains, sends[0], *(crossed(sends[at], at, 0) for at in (2, 3, 1)),
    )
    outputs, token = call(
        outputs_kernel, [(64, 1024), (8, SIDE)], out_own, swapped(out_far, "chan", 2)
    )
    grad_mix, grad_conv, grad_skip, grad_inputs, token = call(
        final_kernel, [(64, 256), (3, 64), (1, 4), (64, 1024), (8, SIDE)],
        gains, grad_out, sends[0], *(crossed(sends[at], at, 1) for at in (2, 3, 1)),
        scratch=[(512, SIDE)], after=[token],
    )
    grad_kernel = call(
        finish_kernel, [(4, LENGTH)], kernel_local, swapped(kernel_local, "dp", 1)
    )
    return (outputs[None], grad_inputs[None], grad_kernel, grad_skip[0], grad_mix.T, grad_conv)


def solution(mesh):
    placed = (
        P("dp", "chan", "seq"),
        P("dp", "chan", "seq"),
        P(None, "chan"),
        P(("chan", "seq"), None),
        P(("chan", "seq")),
        P(None, "chan"),
    )
    return jax.shard_map(
        shards,
        mesh=mesh,
        in_specs=placed,
        out_specs=(
            P("dp", "chan", "seq"),
            P("dp", "chan", "seq"),
            P(("chan", "seq"), None),
            P(("chan", "seq")),
            P(None, "chan"),
            P(None, "chan"),
        ),
        check_vma=False,
    )
```
